32 devices in a mesh: group: 4 (over y, x), member: 8 (over z, core).
Axes of the slice: x: 2, y: 2, z: 4, core: 2. Of those that a mesh axis runs over, the one named last changes fastest.
Arguments:
- features: bfloat16 [32768, 1024], P(('group', 'member')), may hold values from -6 to 6
- w_self: bfloat16 [1024, 1024], replicated, may hold values from -0.1875 to 0.1875
- w_neigh: bfloat16 [1024, 1024], replicated, may hold values from -0.1875 to 0.1875
- bias: bfloat16 [1024], replicated, may hold values from -3 to 3
- hub_rows: int32 [192], P(('group', 'member')), may hold values from 0 to 1023
- hub_nbrs: int32 [32768, 8], P(('group', 'member')), may hold values from 0 to 191
- local_nbrs: int32 [32768, 16], P(('group', 'member')), may hold values from 0 to 1023
- halo_nbrs: int32 [32768, 16], P(('group', 'member')), may hold values from 0 to 1023
- degrees: int32 [3, 32768], P(None, ('group', 'member')), may hold values from 0 to 16, as said below
- send_rows: int32 [32, 8, 128], P(('group', 'member')), may hold values from 0 to 1023
Outputs:
- hidden_out: bfloat16 [32768, 1024], P(('group', 'member'))
The draws below stay inside these ranges and needn't reach their ends.
Inputs may be any that keep to these rules, and one draw needn't show every extreme that they name: degrees[0] is at least 1 and reaches 16; degrees[1] reaches 8; degrees[2] reaches 16, each in every draw.
All inputs are finite; a program needn't handle non-finite values.
Results may differ from the reference program's by a relative error of at most 0.002.
Values may be sent and summed in bfloat16 or wider, within the bound.
No kernel may reach another device: no remote copies, remote signals or barrier semaphores. Data moves between devices by JAX's collectives and lax.ppermute only.
A program may use at most 128 MiB of HBM per device.

```python
import math
import jax
import jax.numpy as jnp
from jax import lax

D_IN = 1024
D_OUT = 1024
ROWS = 1024
HUB_DEV = 6
CAP = 128
KL = 16
KH = 8
KR = 16
PEERS = 8
NDEV = 32
NODES = 32768
HUBS = 192


def draw_degrees(key, part):
    first, second, third = jax.random.split(key, 3)
    position = jnp.arange(NODES)
    local_part = jax.random.randint(first, (NODES,), 1, KL + 1)
    local_part = jnp.where(position % ROWS == 0, KL, local_part)
    hub_part = jax.random.randint(second, (NODES,), 0, KH + 1)
    hub_part = jnp.where(position % ROWS == 1, KH, hub_part)
    halo_part = jax.random.randint(third, (NODES,), 0, KR + 1)
    halo_part = jnp.where(position % ROWS == 2, KR, halo_part)
    return jnp.stack([local_part, hub_part, halo_part]).astype(jnp.int32)


def set_ends(values, key, smallest, high):
    extent = values.shape
    index_at = [jax.random.randint(jax.random.fold_in(key, axis), (), 0, extent[axis]) for axis in range(len(extent))]
    values = values.at[tuple(index_at)].set(smallest)
    longest = extent.index(max(extent))
    index_at[longest] = (index_at[longest] + 1) % extent[longest]
    return values.at[tuple(index_at)].set(high)


def steps_of(rng, shape, cuts, low, high):
    loudness, own = 1.0, jax.random.fold_in(rng, 6)
    for dim, blocks in cuts:
        draws = jnp.exp(jax.random.uniform(jax.random.fold_in(own, dim), (blocks,), jnp.float32, low / len(cuts), high / len(cuts)))
        loudness = loudness * jnp.repeat(draws, shape[dim] // blocks).reshape([-1 if axis == dim else 1 for axis in range(len(shape))])
    return loudness


def gaussian(key, shape, spread, reach, cuts=(), kind=jnp.bfloat16):
    loudness = steps_of(key, shape, cuts, -0.22, 0.18) if cuts else 1.0
    array = jax.random.normal(key, shape, jnp.float32) * spread * loudness
    return jnp.minimum(jnp.maximum(array, -reach), reach).astype(kind)


def setup_inputs(seed: int = 0) -> dict:
    seeds = jax.random.split(jax.random.key(seed), 11)
    features = gaussian(seeds[0], (NODES, D_IN), 1.0, 6.0, ((0, 32),))
    w_self = gaussian(seeds[1], (D_IN, D_OUT), D_IN ** -0.5, 0.1875)
    w_neigh = gaussian(seeds[2], (D_IN, D_OUT), D_IN ** -0.5, 0.1875)
    bias = gaussian(seeds[3], (D_OUT,), 0.5, 3.0)
    hub_rows = set_ends(jax.random.randint(seeds[4], (HUBS,), 0, ROWS), jax.random.fold_in(seeds[4], 1), 0, ROWS - 1).astype(jnp.int32)
    hub_nbrs = set_ends(jax.random.randint(seeds[5], (NODES, KH), 0, HUBS), jax.random.fold_in(seeds[5], 1), 0, HUBS - 1).astype(jnp.int32)
    local_nbrs = set_ends(jax.random.randint(seeds[6], (NODES, KL), 0, ROWS), jax.random.fold_in(seeds[6], 1), 0, ROWS - 1).astype(jnp.int32)
    halo_nbrs = set_ends(jax.random.randint(seeds[7], (NODES, KR), 0, PEERS * CAP), jax.random.fold_in(seeds[7], 1), 0, (PEERS * CAP) - 1).astype(jnp.int32)
    degrees = draw_degrees(jax.random.fold_in(seeds[10], 71), 0)
    send_rows = set_ends(jax.random.randint(seeds[9], (NDEV, PEERS, CAP), 0, ROWS), jax.random.fold_in(seeds[9], 1), 0, ROWS - 1).astype(jnp.int32)
    return {"features": features, "w_self": w_self, "w_neigh": w_neigh, "bias": bias, "hub_rows": hub_rows, "hub_nbrs": hub_nbrs, "local_nbrs": local_nbrs, "halo_nbrs": halo_nbrs, "degrees": degrees, "send_rows": send_rows}


def block_mean(self_features, hub_lookup_matrix, neighbour_positions, local_index_list, hub_index_list, halo_index_list, deg):
    local_valid_mask = (jnp.arange(KL)[None, :] < deg[0][:, None]).astype(jnp.float32)
    hub_valid_mask = (jnp.arange(KH)[None, :] < deg[1][:, None]).astype(jnp.float32)
    halo_valid_mask = (jnp.arange(KR)[None, :] < deg[2][:, None]).astype(jnp.float32)
    neighbour_sum = jnp.einsum("xs,xst->xt", local_valid_mask, self_features[local_index_list].astype(jnp.float32))
    neighbour_sum = neighbour_sum + jnp.einsum("xs,xst->xt", hub_valid_mask, hub_lookup_matrix[hub_index_list].astype(jnp.float32))
    neighbour_sum = neighbour_sum + jnp.einsum("xs,xst->xt", halo_valid_mask, neighbour_positions[halo_index_list].astype(jnp.float32))
    count = jnp.sum(local_valid_mask, axis=1) + jnp.sum(hub_valid_mask, axis=1) + jnp.sum(halo_valid_mask, axis=1)
    return (neighbour_sum / count[:, None]).astype(jnp.bfloat16)


def reference(features, w_self, w_neigh, bias, hub_rows, hub_nbrs, local_nbrs, halo_nbrs, degrees, send_rows):
    owner = (jnp.arange(HUBS) // HUB_DEV).astype(jnp.int32)
    hub_lookup_matrix = features[owner * ROWS + hub_rows]
    blk = math.gcd(ROWS, 256)

    def per_device(dev):
        start = (dev * ROWS).astype(jnp.int32)
        self_features = lax.dynamic_slice_in_dim(features, start, ROWS, 0)
        grp = dev // PEERS
        mem = dev % PEERS
        sources = (grp * PEERS + jnp.arange(PEERS)).astype(jnp.int32)
        rows = send_rows[sources, mem]
        neighbour_positions = features[(sources * ROWS)[:, None] + rows].reshape(PEERS * CAP, D_IN)
        local_index_list = lax.dynamic_slice_in_dim(local_nbrs, start, ROWS, 0).reshape(ROWS // blk, blk, KL)
        hub_index_list = lax.dynamic_slice_in_dim(hub_nbrs, start, ROWS, 0).reshape(ROWS // blk, blk, KH)
        halo_index_list = lax.dynamic_slice_in_dim(halo_nbrs, start, ROWS, 0).reshape(ROWS // blk, blk, KR)
        deg = lax.dynamic_slice_in_dim(degrees, start, ROWS, 1).reshape(3, ROWS // blk, blk).transpose(1, 0, 2)

        def one(item):
            return block_mean(self_features, hub_lookup_matrix, neighbour_positions, item[0], item[1], item[2], item[3])

        means = lax.map(one, (local_index_list, hub_index_list, halo_index_list, deg))
        neigh_mean = means.reshape(ROWS, D_IN)
        value = jnp.dot(self_features, w_self, preferred_element_type=jnp.float32)
        value = value + jnp.dot(neigh_mean, w_neigh, preferred_element_type=jnp.float32)
        value = value + bias.astype(jnp.float32)[None, :]
        return jnp.maximum(value, 0.0).astype(jnp.bfloat16)

    outs = lax.map(per_device, jnp.arange(NDEV, dtype=jnp.int32))
    return outs.reshape(NODES, D_OUT)
```

```python
import functools

import jax
import jax.numpy as jnp
from jax import lax
from jax.experimental import pallas as pl
from jax.experimental.pallas import tpu as pltpu
from jax.sharding import PartitionSpec as P

LANES = 128
HUB_PAD = 8
VM = pl.BlockSpec(memory_space=pltpu.VMEM)
SM = pl.BlockSpec(memory_space=pltpu.SMEM)


def call(kernel, out_shape, in_specs, limit, flops, bytes_accessed):
    single = not isinstance(out_shape, (list, tuple))
    return pl.pallas_call(
        kernel,
        out_shape=out_shape,
        in_specs=in_specs,
        out_specs=VM if single else [VM] * len(out_shape),
        compiler_params=pltpu.CompilerParams(vmem_limit_bytes=limit),
        cost_estimate=pl.CostEstimate(flops=flops, bytes_accessed=bytes_accessed, transcendentals=0),
    )


def gather_kernel(shifts, with_hub, splits, me_ref, rows_ref, hub_ref, feat_ref, *out_refs):
    me = me_ref[0]
    rows_here = feat_ref.shape[0]
    caps = rows_ref.shape[1]
    picks = []
    if with_hub:
        row_at = lax.broadcasted_iota(jnp.int32, (16, rows_here), 1)
        line = lax.broadcasted_iota(jnp.int32, (16, rows_here), 0)
        hit = jnp.zeros((16, rows_here), jnp.float32)
        for h in range(hub_ref.shape[0]):
            hit = hit + jnp.where((line == h) & (row_at == hub_ref[h]), 1.0, 0.0)
        picks.append(hit.astype(jnp.bfloat16))
    row_at = lax.broadcasted_iota(jnp.int32, (caps, rows_here), 1)
    for shift in shifts:
        wanted = rows_ref[pl.ds(me ^ shift, 1), :]
        wanted = jnp.transpose(jnp.broadcast_to(wanted, (8, caps)))[:, :1]
        picks.append(jnp.where(row_at == wanted, 1.0, 0.0).astype(jnp.bfloat16))
    picked = jnp.dot(
        jnp.concatenate(picks, axis=0), feat_ref[...], preferred_element_type=jnp.float32
    ).astype(jnp.bfloat16)
    at = 0
    out = 0
    if with_hub:
        out_refs[0][...] = picked[:HUB_PAD]
        at, out = 16, 1
    for shift in shifts:
        block = picked[at : at + caps]
        at += caps
        parts = splits.get(shift, 1)
        width = block.shape[1] // parts
        for part in range(parts):
            out_refs[out][...] = block[:, part * width : (part + 1) * width]
            out += 1


def add_counts(index, valid, offset, width, out_ref, row, column):
    rb, kmax = index.shape
    slot = lax.broadcasted_iota(jnp.int32, index.shape, 1)
    index = jnp.where(slot < valid, index, -1).astype(jnp.int16)
    columns = [jnp.broadcast_to(index[:, k : k + 1], (rb, LANES)) for k in range(kmax)]
    lane = lax.broadcasted_iota(jnp.int32, (rb, LANES), 1).astype(jnp.int16)
    one = jnp.ones((rb, LANES), jnp.bfloat16)
    zero = jnp.zeros((rb, LANES), jnp.bfloat16)
    for g in range(width // LANES):
        number = lane + jnp.asarray(offset + g * LANES, jnp.int16)
        total = zero
        for k in range(kmax):
            total = total + jnp.where(columns[k] == number, one, zero)
        out_ref[pl.ds(row, rb), column + g * LANES : column + (g + 1) * LANES] = total


def table_kernel(rb, peers, local_ref, hub_ref, halo_ref, deg_ref, local_out, hub_out, halo_out):
    def body(i, carry):
        row = pl.multiple_of(i * rb, rb)
        deg = deg_ref[pl.ds(row, rb), :]
        add_counts(local_ref[pl.ds(row, rb), :], deg[:, 0:1], 0, local_out.shape[1], local_out, row, 0)
        add_counts(hub_ref[pl.ds(row, rb), :], deg[:, 1:2], 0, hub_out.shape[1], hub_out, row, 0)
        add_counts(halo_ref[pl.ds(row, rb), :], deg[:, 2:3], 0, halo_out.shape[1], halo_out, row, 0)
        return carry

    lax.fori_loop(0, local_ref.shape[0] // rb, body, 0)


def own_kernel(rb, feat_ref, w_ref, bias_ref, out_ref):
    bias = bias_ref[...].astype(jnp.float32)

    def body(i, carry):
        row = pl.multiple_of(i * rb, rb)
        out_ref[pl.ds(row, rb), :] = (
            jnp.dot(feat_ref[pl.ds(row, rb), :], w_ref[...], preferred_element_type=jnp.float32) + bias
        )
        return carry

    lax.fori_loop(0, feat_ref.shape[0] // rb, body, 0)


def sum_kernel(rb, count, local_ref, hub_ref, halo_ref, feat_ref, table_ref, *refs):
    blocks, out_ref = refs[:count], refs[count]
    caps = blocks[0].shape[0]

    def body(i, carry):
        row = pl.multiple_of(i * rb, rb)
        total = jnp.dot(local_ref[pl.ds(row, rb), :], feat_ref[...], preferred_element_type=jnp.float32)
        total = total + jnp.dot(hub_ref[pl.ds(row, rb), :], table_ref[...], preferred_element_type=jnp.float32)
        for b in range(count):
            total = total + jnp.dot(
                halo_ref[pl.ds(row, rb), b * caps : (b + 1) * caps],
                blocks[b][...],
                preferred_element_type=jnp.float32,
            )
        out_ref[pl.ds(row, rb), :] = total
        return carry

    lax.fori_loop(0, local_ref.shape[0] // rb, body, 0)


def last_kernel(rb, parts, sum_ref, own_ref, halo_ref, deg_ref, w_ref, *refs):
    blocks, out_ref = refs[:parts], refs[parts]
    caps = blocks[0].shape[0]
    width = blocks[0].shape[1]
    at = halo_ref.shape[1] - caps

    def body(i, carry):
        row = pl.multiple_of(i * rb, rb)
        deg = deg_ref[pl.ds(row, rb), :]
        scale = 1.0 / (deg[:, 0:1] + deg[:, 1:2] + deg[:, 2:3]).astype(jnp.float32)
        value = own_ref[pl.ds(row, rb), :]
        for part in range(parts):
            span = slice(part * width, (part + 1) * width)
            total = sum_ref[pl.ds(row, rb), span] + jnp.dot(
                halo_ref[pl.ds(row, rb), at:], blocks[part][...], preferred_element_type=jnp.float32
            )
            mean = (total * scale).astype(jnp.bfloat16)
            value = value + jnp.dot(mean, w_ref[span, :], preferred_element_type=jnp.float32)
        out_ref[pl.ds(row, rb), :] = jnp.maximum(value, 0.0).astype(jnp.bfloat16)
        return carry

    lax.fori_loop(0, sum_ref.shape[0] // rb, body, 0)


def per_device(groups, features, w_self, w_neigh, bias, hub_rows, hub_nbrs, local_nbrs, halo_nbrs, degrees, send_rows):
    rows_here, width = features.shape
    peers, caps = send_rows.shape[1:]
    hub_dev = hub_rows.shape[0]
    bf16, f32 = jnp.bfloat16, jnp.float32
    me = lax.axis_index("member")
    group = lax.axis_index("group")
    me_arr = me.reshape(1).astype(jnp.int32)
    rows = send_rows.reshape(peers, caps)

    order = list(range(peers // 2, peers - 1)) + list(range(1, peers // 2)) + [0, peers - 1]
    early, late = order[:-1], order[-1]
    splits = {late: 2}

    def gather(shifts, with_hub):
        outs = [jax.ShapeDtypeStruct((HUB_PAD, width), bf16)] if with_hub else []
        for shift in shifts:
            parts = splits.get(shift, 1)
            outs += [jax.ShapeDtypeStruct((caps, width // parts), bf16)] * parts
        return call(
            functools.partial(gather_kernel, shifts, with_hub, splits),
            outs,
            [SM, VM, SM, VM],
            24 << 20,
            2 * len(shifts) * caps * rows_here * width,
            2 * rows_here * width + 2 * len(shifts) * caps * width,
        )(me_arr, rows, hub_rows, features)

    def swap(block, axis, size, shift):
        return lax.ppermute(block, axis, [(i, i ^ shift) for i in range(size)])

    first = gather(order[:1], True)
    hubs, sent = first[0], {order[0]: first[1:]}
    rest = gather(order[1:], False)
    at = 0
    for shift in order[1:]:
        parts = splits.get(shift, 1)
        sent[shift] = rest[at : at + parts]
        at += parts
    got = {}
    for shift in order:
        got[shift] = sent[shift] if shift == 0 else [swap(b, "member", peers, shift) for b in sent[shift]]

    bits = [("member", 1 << b) for b in range(1, peers.bit_length() - 1)]
    bits += [("group", 1 << b) for b in range(groups.bit_length() - 1)]
    bits += [("member", 1)]
    distance = {"member": jnp.int32(0), "group": jnp.int32(0)}
    owner = hub_nbrs // hub_dev
    apart = {"member": (owner % peers) ^ me, "group": (owner // peers) ^ group}
    block_at = jnp.zeros_like(hub_nbrs)
    for n, (axis, bit) in enumerate(bits):
        other = swap(hubs, axis, peers if axis == "member" else groups, bit)
        hubs = jnp.concatenate([hubs, other], axis=0)
        block_at = block_at + jnp.where((apart[axis] & bit) != 0, 1 << n, 0)
    hub_index = block_at * HUB_PAD + hub_nbrs % hub_dev
    halo_apart = (halo_nbrs // caps) ^ me
    halo_place = jnp.zeros_like(halo_nbrs)
    for n, shift in enumerate(order):
        halo_place = jnp.where(halo_apart == shift, n, halo_place)
    halo_index = halo_place * caps + halo_nbrs % caps
    deg = degrees.T

    hub_slots = hubs.shape[0]
    halo_slots = peers * caps
    local_counts, hub_counts, halo_counts = call(
        functools.partial(table_kernel, 64, peers),
        [
            jax.ShapeDtypeStruct((rows_here, rows_here), bf16),
            jax.ShapeDtypeStruct((rows_here, hub_slots), bf16),
            jax.ShapeDtypeStruct((rows_here, halo_slots), bf16),
        ],
        [VM] * 4,
        32 << 20,
        24 * rows_here * (rows_here + halo_slots),
        2 * rows_here * (rows_here + hub_slots + halo_slots),
    )(local_nbrs, hub_index, halo_index, deg)

    own = call(
        functools.partial(own_kernel, 256),
        jax.ShapeDtypeStruct((rows_here, width), f32),
        [VM] * 3,
        32 << 20,
        2 * rows_here * width * width,
        8 * rows_here * width,
    )(features, w_self, bias.reshape(1, width))

    total = call(
        functools.partial(sum_kernel, 256, len(early)),
        jax.ShapeDtypeStruct((rows_here, width), f32),
        [VM] * (5 + len(early)),
        40 << 20,
        2 * rows_here * width * (rows_here + hub_slots + halo_slots),
        8 * rows_here * width,
    )(local_counts, hub_counts, halo_counts, features, hubs, *[got[s][0] for s in early])

    return call(
        functools.partial(last_kernel, 256, splits[late]),
        jax.ShapeDtypeStruct((rows_here, width), bf16),
        [VM] * (5 + splits[late]),
        40 << 20,
        2 * rows_here * width * (width + caps),
        8 * rows_here * width,
    )(total, own, halo_counts, deg, w_neigh, *got[late])


def solution(mesh):
    both = ("group", "member")
    in_specs = (
        P(both, None),
        P(),
        P(),
        P(),
        P(both),
        P(both, None),
        P(both, None),
        P(both, None),
        P(None, both),
        P(both, None, None),
    )
    return jax.shard_map(
        functools.partial(per_device, mesh.shape["group"]),
        mesh=mesh,
        in_specs=in_specs,
        out_specs=P(both, None),
        check_vma=False,
    )
```

```python
import functools

import jax
import jax.numpy as jnp
from jax import lax
from jax.experimental import pallas as pl
from jax.experimental.pallas import tpu as pltpu
from jax.sharding import PartitionSpec as P

LANES = 128
HUB_PAD = 8
VM = pl.BlockSpec(memory_space=pltpu.VMEM)
ANY = pl.BlockSpec(memory_space=pl.ANY)
SM = pl.BlockSpec(memory_space=pltpu.SMEM)
BF, F32 = jnp.bfloat16, jnp.float32


def call(kernel, out_shape, in_specs, limit, flops, bytes_accessed, scratch=(), out_specs=None, aliases=None):
    single = not isinstance(out_shape, (list, tuple))
    return pl.pallas_call(
        kernel,
        out_shape=out_shape,
        in_specs=in_specs,
        out_specs=out_specs or (VM if single else [VM] * len(out_shape)),
        scratch_shapes=list(scratch),
        input_output_aliases=aliases or {},
        compiler_params=pltpu.CompilerParams(vmem_limit_bytes=limit),
        cost_estimate=pl.CostEstimate(flops=flops, bytes_accessed=bytes_accessed, transcendentals=0),
    )


def column_of(row, rows):
    return jnp.transpose(jnp.broadcast_to(row, (8, rows)))[:, :1]


def pick_matrix(rows_ref, shift, rows_here):
    me = lax.axis_index("member")
    caps = rows_ref.shape[1]
    wanted = column_of(rows_ref[pl.ds(me ^ shift, 1), :], caps)
    row_at = lax.broadcasted_iota(jnp.int32, (caps, rows_here), 1)
    return jnp.where(row_at == wanted, 1.0, 0.0).astype(BF)


def hub_matrix(hub_ref, rows_here):
    row_at = lax.broadcasted_iota(jnp.int32, (HUB_PAD, rows_here), 1)
    line = lax.broadcasted_iota(jnp.int32, (HUB_PAD, rows_here), 0)
    hit = jnp.zeros((HUB_PAD, rows_here), F32)
    for h in range(hub_ref.shape[0]):
        hit = hit + jnp.where((line == h) & (row_at == hub_ref[h]), 1.0, 0.0)
    return hit.astype(BF)


def first_kernel(shifts, chunks, rows_hbm, hub_hbm, feat_hbm, *refs):
    outs, hub_out = refs[: len(shifts)], refs[len(shifts)]
    rows_ref, hub_ref, feat_ref, sems = refs[len(shifts) + 1 :]
    rows_here = feat_ref.shape[0]
    part = rows_here // chunks
    copies = [
        pltpu.make_async_copy(rows_hbm, rows_ref, sems.at[0]),
        pltpu.make_async_copy(hub_hbm, hub_ref, sems.at[1]),
    ]
    for c in range(chunks):
        span = pl.ds(c * part, part)
        copies.append(pltpu.make_async_copy(feat_hbm.at[span, :], feat_ref.at[span, :], sems.at[2 + c]))
    for copy in copies:
        copy.start()
    copies[0].wait()
    copies[1].wait()
    picks = [pick_matrix(rows_ref, shift, rows_here) for shift in shifts]
    picks.append(hub_matrix(hub_ref, rows_here))
    for copy in copies[2:]:
        copy.wait()
    caps = rows_ref.shape[1]
    picked = jnp.dot(jnp.concatenate(picks, axis=0), feat_ref[...], preferred_element_type=F32).astype(BF)
    hubs = picked[len(shifts) * caps :]
    hub_out[...] = hubs
    for n in range(len(shifts)):
        outs[n][...] = jnp.concatenate([picked[n * caps : (n + 1) * caps], hubs], axis=0)


def rest_kernel(shifts, parts, rows_ref, feat_ref, *outs):
    rows_here, width = feat_ref.shape
    caps = rows_ref.shape[1]
    picks = [pick_matrix(rows_ref, shift, rows_here) for shift in shifts]
    picked = jnp.dot(jnp.concatenate(picks, axis=0), feat_ref[...], preferred_element_type=F32).astype(BF)
    for n in range(len(shifts) - 1):
        outs[n][...] = picked[n * caps : (n + 1) * caps]
    for p in range(parts):
        outs[len(shifts) - 1 + p][...] = picked[-caps:, p * (width // parts) : (p + 1) * (width // parts)]


def join_kernel(caps, *refs):
    out_ref = refs[-1]
    at = 0
    for ref in refs[:-1]:
        start = caps if ref.shape[0] == caps + HUB_PAD else 0
        size = ref.shape[0] - start
        out_ref[at : at + size, :] = ref[start:, :]
        at += size


def add_counts(index, width, out_ref, row, column):
    rb, kmax = index.shape
    index = index.astype(jnp.int16)
    columns = [jnp.broadcast_to(index[:, k : k + 1], (rb, LANES)) for k in range(kmax)]
    lane = lax.broadcasted_iota(jnp.int32, (rb, LANES), 1).astype(jnp.int16)
    one = jnp.ones((rb, LANES), BF)
    zero = jnp.zeros((rb, LANES), BF)
    for g in range(width // LANES):
        number = lane + jnp.asarray(g * LANES, jnp.int16)
        total = zero
        for k in range(kmax):
            total = total + jnp.where(columns[k] == number, one, zero)
        out_ref[pl.ds(row, rb), column + g * LANES : column + (g + 1) * LANES] = total


def table_kernel(rb, peers, caps, hub_dev, magic, local_ref, hub_ref, halo_ref, deg_ref, out_ref):
    me = lax.axis_index("member")
    group = lax.axis_index("group")
    rows_here = local_ref.shape[1]
    halo_slots = peers * caps
    hub_slots = out_ref.shape[1] - rows_here - halo_slots
    near = hub_slots // (2 * HUB_PAD)
    half = peers // 2

    def body(i, carry):
        row = pl.multiple_of(i * rb, rb)
        span = pl.ds(row, rb)

        def masked(ref, which, index):
            slot = lax.broadcasted_iota(jnp.int32, index.shape, 0)
            index = jnp.where(slot < deg_ref[which : which + 1, span], index, -1)
            return jnp.transpose(index)

        local = masked(local_ref, 0, local_ref[:, span])
        hub = hub_ref[:, span]
        owner = (hub * magic) >> 16
        apart = (owner & (peers - 1)) ^ me
        line = (owner >> (peers.bit_length() - 1)) ^ group
        place = (apart & 1) * near + line * half + (apart >> 1)
        hub = masked(hub_ref, 1, place * HUB_PAD + hub - owner * hub_dev)
        halo = masked(halo_ref, 2, halo_ref[:, span] ^ (me * caps))
        add_counts(local, rows_here, out_ref, row, 0)
        add_counts(hub, hub_slots, out_ref, row, rows_here)
        add_counts(halo, halo_slots, out_ref, row, rows_here + hub_slots)
        return carry

    lax.fori_loop(0, rows_here // rb, body, 0)


def own_kernel(rb, feat_ref, w_ref, bias_ref, count_ref, own_ref, sum_ref):
    bias = bias_ref[...].astype(F32)
    rows_here = feat_ref.shape[0]

    def body(i, carry):
        span = pl.ds(pl.multiple_of(i * rb, rb), rb)
        own_ref[span, :] = jnp.dot(feat_ref[span, :], w_ref[...], preferred_element_type=F32) + bias
        sum_ref[span, :] = jnp.dot(count_ref[span, :rows_here], feat_ref[...], preferred_element_type=F32)
        return carry

    lax.fori_loop(0, rows_here // rb, body, 0)


def sum_kernel(rb, caps, blocks, sum_ref, count_ref, *refs):
    parts, out_ref, joined = refs[:blocks], refs[blocks], refs[blocks + 1]
    rows_here = sum_ref.shape[0]
    at = 0
    for ref in parts:
        size = caps if ref.shape[0] == caps + HUB_PAD else ref.shape[0]
        joined[at : at + size, :] = ref[:size, :]
        at += size

    def body(i, carry):
        span = pl.ds(pl.multiple_of(i * rb, rb), rb)
        out_ref[span, :] = sum_ref[span, :] + jnp.dot(
            count_ref[span, rows_here : rows_here + at], joined[...], preferred_element_type=F32
        )
        return carry

    lax.fori_loop(0, rows_here // rb, body, 0)


def mean_part(span, cols, sum_ref, count_ref, deg_ref, block_ref, w_ref, value):
    caps = block_ref.shape[0]
    deg = deg_ref[0:1, span] + deg_ref[1:2, span] + deg_ref[2:3, span]
    scale = column_of(1.0 / deg.astype(F32), deg.shape[1])
    at = count_ref.shape[1] - caps
    total = sum_ref[span, cols] + jnp.dot(count_ref[span, at:], block_ref[...], preferred_element_type=F32)
    mean = (total * scale).astype(BF)
    return value + jnp.dot(mean, w_ref[cols, :], preferred_element_type=F32)


def late_kernel(rb, cols, own_ref, sum_ref, count_ref, deg_ref, w_ref, block_ref, out_ref):
    def body(i, carry):
        span = pl.ds(pl.multiple_of(i * rb, rb), rb)
        out_ref[span, :] = mean_part(span, cols, sum_ref, count_ref, deg_ref, block_ref, w_ref, own_ref[span, :])
        return carry

    lax.fori_loop(0, sum_ref.shape[0] // rb, body, 0)


def last_kernel(rb, cols, own_ref, sum_ref, count_ref, deg_ref, w_ref, block_ref, out_hbm, out_ref, sems):
    steps = sum_ref.shape[0] // rb
    copies = []
    for i in range(steps):
        span = pl.ds(i * rb, rb)
        value = mean_part(span, cols, sum_ref, count_ref, deg_ref, block_ref, w_ref, own_ref[span, :])
        out_ref[span, :] = jnp.maximum(value, 0.0).astype(BF)
        copies.append(pltpu.make_async_copy(out_ref.at[span, :], out_hbm.at[span, :], sems.at[i]))
        copies[-1].start()
    for copy in copies:
        copy.wait()


def per_device(groups, features, w_self, w_neigh, bias, hub_rows, hub_nbrs, local_nbrs, halo_nbrs, degrees, send_rows):
    rows_here, width = features.shape
    peers, caps = send_rows.shape[1:]
    hub_dev = hub_rows.shape[0]
    hubs_all = hub_dev * peers * groups
    magic = -(-(1 << 16) // hub_dev)
    assert all((h * magic) >> 16 == h // hub_dev for h in range(hubs_all))
    assert peers & (peers - 1) == 0 and groups & (groups - 1) == 0
    rows = send_rows.reshape(peers, caps)
    vec = functools.partial(jax.ShapeDtypeStruct)

    evens = [s for s in range(peers // 2, peers, 2)] + [s for s in range(2, peers // 2, 2)]
    last = peers - 1
    odds = [s for s in range(peers // 2 + 1, peers - 1, 2)] + [s for s in range(1, peers // 2, 2)]
    parts = 2

    def swap(block, axis, shift):
        size = peers if axis == "member" else groups
        return lax.ppermute(block, axis, [(i, i ^ shift) for i in range(size)])

    chunks = 4
    firsts = call(
        functools.partial(first_kernel, evens, chunks),
        [vec((caps + HUB_PAD, width), BF)] * len(evens) + [vec((HUB_PAD, width), BF)],
        [ANY] * 3,
        16 << 20,
        2 * len(evens) * caps * rows_here * width,
        2 * rows_here * width,
        scratch=[
            pltpu.VMEM((peers, caps), jnp.int32),
            pltpu.SMEM((hub_dev,), jnp.int32),
            pltpu.VMEM((rows_here, width), BF),
            pltpu.SemaphoreType.DMA((2 + chunks,)),
        ],
    )(rows, hub_rows, features)
    got = {shift: swap(block, "member", shift) for shift, block in zip(evens, firsts)}
    others = odds + [0, last]
    rest = call(
        functools.partial(rest_kernel, others, parts),
        [vec((caps, width), BF)] * (len(others) - 1) + [vec((caps, width // parts), BF)] * parts,
        [VM] * 2,
        16 << 20,
        2 * len(others) * caps * rows_here * width,
        2 * rows_here * width,
    )(rows, features)
    for shift, block in zip(odds, rest):
        got[shift] = swap(block, "member", shift)
    got[0] = rest[len(odds)]
    late = [swap(block, "member", last) for block in rest[len(odds) + 1 :]]

    def join(*blocks):
        total = sum(HUB_PAD if b.shape[0] == caps + HUB_PAD else b.shape[0] for b in blocks)
        return call(
            functools.partial(join_kernel, caps), vec((total, width), BF), [VM] * len(blocks), 4 << 20, 0, 4 * total * width
        )(*blocks)

    hubs = join(firsts[-1], *[got[s] for s in range(2, peers, 2)])
    for bit in range(groups.bit_length() - 1):
        hubs = join(hubs, swap(hubs, "group", 1 << bit))
    other_hubs = swap(hubs, "member", 1)

    hub_slots = 2 * hubs.shape[0]
    counts = call(
        functools.partial(table_kernel, LANES, peers, caps, hub_dev, magic),
        vec((rows_here, rows_here + hub_slots + peers * caps), BF),
        [VM] * 4,
        16 << 20,
        24 * rows_here * (rows_here + peers * caps),
        2 * rows_here * (rows_here + hub_slots + peers * caps),
    )(local_nbrs.T, hub_nbrs.T, halo_nbrs.T, degrees)

    own, local_sum = call(
        functools.partial(own_kernel, 256),
        [vec((rows_here, width), F32)] * 2,
        [VM] * 4,
        16 << 20,
        4 * rows_here * width * width,
        8 * rows_here * width,
    )(features, w_self, bias.reshape(1, width), counts)

    early = [hubs, other_hubs] + [got[s] for s in range(last)]
    total = call(
        functools.partial(sum_kernel, 256, caps, len(early)),
        vec((rows_here, width), F32),
        [VM] * (2 + len(early)),
        16 << 20,
        2 * rows_here * width * (hub_slots + last * caps),
        8 * rows_here * width,
        scratch=[pltpu.VMEM((hub_slots + last * caps, width), BF)],
    )(local_sum, counts, *early)

    step = width // parts
    value = own
    for p in range(parts - 1):
        value = call(
            functools.partial(late_kernel, 256, slice(p * step, (p + 1) * step)),
            vec((rows_here, width), F32),
            [VM] * 6,
            16 << 20,
            2 * rows_here * step * (width + caps),
            8 * rows_here * width,
        )(value, total, counts, degrees, w_neigh, late[p])
    return call(
        functools.partial(last_kernel, 256, slice((parts - 1) * step, width)),
        vec((rows_here, width), BF),
        [VM] * 6,
        16 << 20,
        2 * rows_here * step * (width + caps),
        8 * rows_here * width,
        scratch=[pltpu.VMEM((rows_here, width), BF), pltpu.SemaphoreType.DMA((rows_here // 256,))],
        out_specs=ANY,
    )(value, total, counts, degrees, w_neigh, late[-1])


def solution(mesh):
    both = ("group", "member")
    in_specs = (
        P(both, None),
        P(),
        P(),
        P(),
        P(both),
        P(both, None),
        P(both, None),
        P(both, None),
        P(None, both),
        P(both, None, None),
    )
    return jax.shard_map(
        functools.partial(per_device, mesh.shape["group"]),
        mesh=mesh,
        in_specs=in_specs,
        out_specs=P(both, None),
        check_vma=False,
    )
```

```python
import functools

import jax
import jax.numpy as jnp
from jax import lax
from jax.experimental import pallas as pl
from jax.experimental.pallas import tpu as pltpu
from jax.sharding import PartitionSpec as P

LANES = 128
HUB_PAD = 8
CHUNKS = 4
VM = pl.BlockSpec(memory_space=pltpu.VMEM)
ANY = pl.BlockSpec(memory_space=pl.ANY)
HBM = pl.BlockSpec(memory_space=pltpu.HBM)
BF, F32, I32 = jnp.bfloat16, jnp.float32, jnp.int32
vec = jax.ShapeDtypeStruct


def call(kernel, out_shape, in_specs, flops, bytes_accessed, limit=16, scratch=(), out_specs=None):
    single = not isinstance(out_shape, (list, tuple))
    return pl.pallas_call(
        kernel,
        out_shape=out_shape,
        in_specs=in_specs,
        out_specs=out_specs or (VM if single else [VM] * len(out_shape)),
        scratch_shapes=list(scratch),
        compiler_params=pltpu.CompilerParams(vmem_limit_bytes=limit << 20),
        cost_estimate=pl.CostEstimate(flops=4 * flops, bytes_accessed=bytes_accessed, transcendentals=0),
    )


def column_of(row, rows):
    return jnp.transpose(jnp.broadcast_to(row, (8, rows)))[:, :1]


def pick_matrix(rows_ref, shift, rows_here):
    me = lax.axis_index("member")
    caps = rows_ref.shape[1]
    wanted = column_of(rows_ref[pl.ds(me ^ shift, 1), :], caps)
    row_at = lax.broadcasted_iota(I32, (caps, rows_here), 1)
    return jnp.where(row_at == wanted, 1.0, 0.0).astype(BF)


def hub_matrix(hub_ref, rows_here):
    row_at = lax.broadcasted_iota(I32, (HUB_PAD, rows_here), 1)
    line = lax.broadcasted_iota(I32, (HUB_PAD, rows_here), 0)
    hit = jnp.zeros((HUB_PAD, rows_here), F32)
    for h in range(hub_ref.shape[0]):
        hit = hit + jnp.where((line == h) & (row_at == hub_ref[h]), 1.0, 0.0)
    return hit.astype(BF)


def load(small, feat_hbm, feat_ref, sems):
    copies = [pltpu.make_async_copy(a, b, sems.at[n]) for n, (a, b) in enumerate(small)]
    part = feat_ref.shape[0] // CHUNKS
    large = []
    for c in range(CHUNKS):
        span = pl.ds(c * part, part)
        large.append(pltpu.make_async_copy(feat_hbm.at[span, :], feat_ref.at[span, :], sems.at[len(small) + c]))
    for copy in copies + large:
        copy.start()
    for copy in copies:
        copy.wait()
    return large


def picked_rows(picks, feat_ref, copies):
    picks = jnp.concatenate(picks, axis=0)
    part = feat_ref.shape[0] // len(copies)
    picked = None
    for c, copy in enumerate(copies):
        copy.wait()
        span = slice(c * part, (c + 1) * part)
        term = jnp.dot(picks[:, span], feat_ref[span, :], preferred_element_type=F32)
        picked = term if picked is None else picked + term
    return picked.astype(BF)


def first_kernel(shifts, rows_hbm, hub_hbm, feat_hbm, *refs):
    outs, hub_out = refs[: len(shifts)], refs[len(shifts)]
    rows_ref, hub_ref, feat_ref, sems = refs[len(shifts) + 1 :]
    large = load([(rows_hbm, rows_ref), (hub_hbm, hub_ref)], feat_hbm, feat_ref, sems)
    rows_here = feat_ref.shape[0]
    caps = rows_ref.shape[1]
    picks = [pick_matrix(rows_ref, shift, rows_here) for shift in shifts]
    picked = picked_rows(picks + [hub_matrix(hub_ref, rows_here)], feat_ref, large)
    hubs = picked[len(shifts) * caps :]
    hub_out[...] = hubs
    for n in range(len(shifts)):
        block = picked[n * caps : (n + 1) * caps]
        outs[n][...] = jnp.concatenate([block, hubs], axis=0) if shifts[n] % 2 == 0 else block


def near_kernel(shifts, rows_hbm, hub_hbm, feat_hbm, after_ref, *refs):
    outs = refs[: len(shifts)]
    rows_ref, hub_ref, feat_ref, sems = refs[len(shifts) :]
    large = load([(rows_hbm, rows_ref), (hub_hbm, hub_ref)], feat_hbm, feat_ref, sems)
    caps = rows_ref.shape[1]
    picked = picked_rows([pick_matrix(rows_ref, shift, feat_ref.shape[0]) for shift in shifts], feat_ref, large)
    for n, shift in enumerate(shifts):
        block = picked[n * caps : (n + 1) * caps]
        outs[n][...] = jnp.concatenate([block, hub_ref[...]], axis=0) if shift and shift % 2 == 0 else block


def rest_kernel(shifts, cols, rows_ref, feat_ref, after_ref, *outs):
    caps = rows_ref.shape[1]
    picks = [pick_matrix(rows_ref, shift, feat_ref.shape[0]) for shift in shifts]
    picked = jnp.dot(jnp.concatenate(picks, axis=0), feat_ref[:, cols], preferred_element_type=F32).astype(BF)
    for n in range(len(shifts)):
        outs[n][...] = picked[n * caps : (n + 1) * caps]


def join_kernel(starts, *refs):
    out_ref = refs[-1]
    at = 0
    for start, ref in zip(starts, refs):
        size = ref.shape[0] - start
        out_ref[at : at + size, :] = ref[start:, :]
        at += size


def add_counts(index, width, out_ref, row, column):
    rb, kmax = index.shape
    index = index.astype(jnp.int16)
    columns = [jnp.broadcast_to(index[:, k : k + 1], (rb, LANES)) for k in range(kmax)]
    lane = lax.broadcasted_iota(I32, (rb, LANES), 1).astype(jnp.int16)
    one = jnp.ones((rb, LANES), BF)
    zero = jnp.zeros((rb, LANES), BF)
    for g in range(width // LANES):
        number = lane + jnp.asarray(g * LANES, jnp.int16)
        total = zero
        for k in range(kmax):
            total = total + jnp.where(columns[k] == number, one, zero)
        out_ref[pl.ds(row, rb), column + g * LANES : column + (g + 1) * LANES] = total


def table_kernel(rb, peers, caps, hub_dev, magic, order, local_ref, hub_ref, halo_ref, deg_ref, after_ref, out_ref):
    me = lax.axis_index("member")
    group = lax.axis_index("group")
    rows_here = local_ref.shape[1]
    halo_slots = peers * caps
    hub_slots = out_ref.shape[1] - rows_here - halo_slots
    half = peers // 2

    def body(i, carry):
        row = pl.multiple_of(i * rb, rb)
        span = pl.ds(row, rb)

        def masked(which, index):
            slot = lax.broadcasted_iota(I32, index.shape, 0)
            return jnp.transpose(jnp.where(slot < deg_ref[which : which + 1, span], index, -1))

        local = masked(0, local_ref[:, span])
        hub = hub_ref[:, span]
        owner = (hub * magic) >> 16
        apart = (owner & (peers - 1)) ^ me
        line = (owner >> (peers.bit_length() - 1)) ^ group
        place = (apart & 1) * (hub_slots // (2 * HUB_PAD)) + line * half + (apart >> 1)
        hub = masked(1, place * HUB_PAD + hub - owner * hub_dev)
        slot = halo_ref[:, span]
        apart = (slot >> (caps.bit_length() - 1)) ^ me
        place = apart
        for n, shift in enumerate(order):
            if n != shift:
                place = jnp.where(apart == shift, n, place)
        halo = masked(2, place * caps + (slot & (caps - 1)))
        add_counts(local, rows_here, out_ref, row, 0)
        add_counts(halo, halo_slots, out_ref, row, rows_here)
        add_counts(hub, hub_slots, out_ref, row, rows_here + halo_slots)
        return carry

    lax.fori_loop(0, rows_here // rb, body, 0)


def own_kernel(rb, feat_ref, w_ref, bias_ref, after_ref, out_ref):
    bias = bias_ref[...].astype(F32)
    for i in range(feat_ref.shape[0] // rb):
        span = pl.ds(i * rb, rb)
        out_ref[span, :] = jnp.dot(feat_ref[span, :], w_ref[...], preferred_element_type=F32) + bias


def local_kernel(rb, feat_ref, count_ref, after_ref, out_ref):
    rows_here = feat_ref.shape[0]
    for i in range(rows_here // rb):
        span = pl.ds(i * rb, rb)
        out_ref[span, :] = jnp.dot(count_ref[span, :rows_here], feat_ref[...], preferred_element_type=F32)


def sum_kernel(rb, sizes, at, sum_ref, count_ref, *refs):
    blocks, (_, out_ref, joined) = refs[: len(sizes)], refs[len(sizes) :]
    row = 0
    for size, ref in zip(sizes, blocks):
        joined[row : row + size, :] = ref[:size, :]
        row += size
    for i in range(sum_ref.shape[0] // rb):
        span = pl.ds(i * rb, rb)
        out_ref[span, :] = sum_ref[span, :] + jnp.dot(
            count_ref[span, at : at + row], joined[...], preferred_element_type=F32
        )


def mean_part(span, at, cols, sum_ref, count_ref, deg_ref, w_ref, block_ref, value):
    deg = deg_ref[0:1, span] + deg_ref[1:2, span] + deg_ref[2:3, span]
    scale = column_of(1.0 / deg.astype(F32), deg.shape[1])
    counts = count_ref[span, at : at + block_ref.shape[0]]
    total = sum_ref[span, cols] + jnp.dot(counts, block_ref[...], preferred_element_type=F32)
    mean = (total * scale).astype(BF)
    return value + jnp.dot(mean, w_ref[cols, :], preferred_element_type=F32)


def late_kernel(rb, at, cols, own_ref, sum_ref, count_ref, deg_ref, w_ref, block_ref, out_ref):
    for i in range(sum_ref.shape[0] // rb):
        span = pl.ds(i * rb, rb)
        out_ref[span, :] = mean_part(span, at, cols, sum_ref, count_ref, deg_ref, w_ref, block_ref, own_ref[span, :])


def last_kernel(rb, at, cols, own_ref, sum_ref, count_ref, deg_ref, w_ref, block_ref, out_hbm, out_ref, sems):
    copies = []
    for i in range(sum_ref.shape[0] // rb):
        span = pl.ds(i * rb, rb)
        value = mean_part(span, at, cols, sum_ref, count_ref, deg_ref, w_ref, block_ref, own_ref[span, :])
        out_ref[span, :] = jnp.maximum(value, 0.0).astype(BF)
        copies.append(pltpu.make_async_copy(out_ref.at[span, :], out_hbm.at[span, :], sems.at[i]))
        copies[-1].start()
    for copy in copies:
        copy.wait()


def per_device(groups, features, w_self, w_neigh, bias, hub_rows, hub_nbrs, local_nbrs, halo_nbrs, degrees, send_rows):
    rows_here, width = features.shape
    peers, caps = send_rows.shape[1:]
    hub_dev = hub_rows.shape[0]
    magic = -(-(1 << 16) // hub_dev)
    assert all((h * magic) >> 16 == h // hub_dev for h in range(hub_dev * peers * groups))
    assert peers >= 8 and groups >= 4 and hub_dev <= HUB_PAD
    assert not any(n & (n - 1) for n in (peers, groups, caps))
    rows = send_rows.reshape(peers, caps)
    hub_slots = HUB_PAD * peers * groups

    top, last = peers // 2, peers - 1
    far = list(range(top, last, 2))
    near = list(range(2, top, 2))
    other = list(range(3, last, 2))
    early = [0, 1] + near + far
    order = early + [last] + other
    spans = [slice(0, width - width // 4), slice(width - width // 4, width)]

    def swap(block, axis, shift):
        size = peers if axis == "member" else groups
        return lax.ppermute(block, axis, [(i, i ^ shift) for i in range(size)])

    scratch = [pltpu.VMEM((rows_here, width), BF), pltpu.SemaphoreType.DMA((2 + CHUNKS,))]
    plain, carrier = vec((caps, width), BF), vec((caps + HUB_PAD, width), BF)
    firsts = call(
        functools.partial(first_kernel, far + [1]),
        [carrier] * len(far) + [plain, vec((HUB_PAD, width), BF)],
        [HBM] * 3,
        0,
        2 * rows_here * width,
        limit=60,
        scratch=[pltpu.VMEM((peers, caps), I32), pltpu.SMEM((hub_dev,), I32)] + scratch,
    )(rows, hub_rows, features)
    hubs = firsts[-1]
    got = {shift: swap(block, "member", shift) for shift, block in zip(far + [1], firsts)}
    nears = call(
        functools.partial(near_kernel, near + [0]),
        [plain if shift % 2 else carrier for shift in near] + [plain],
        [HBM] * 3 + [ANY],
        0,
        2 * rows_here * width,
        limit=60,
        scratch=[pltpu.VMEM((peers, caps), I32), pltpu.VMEM((HUB_PAD, width), BF)] + scratch,
    )(rows, hubs, features, got[1])
    for shift, block in zip(near, nears):
        got[shift] = swap(block, "member", shift)
    got[0] = nears[-1]

    counts = call(
        functools.partial(table_kernel, 2 * LANES, peers, caps, hub_dev, magic, order),
        vec((rows_here, rows_here + peers * caps + hub_slots), BF),
        [VM] * 4 + [ANY],
        24 * rows_here * (rows_here + peers * caps),
        2 * rows_here * (rows_here + hub_slots + peers * caps),
    )(local_nbrs.T, hub_nbrs.T, halo_nbrs.T, degrees, got[0])

    def rest(shifts, cols, after):
        return call(
            functools.partial(rest_kernel, shifts, cols),
            [vec((caps, cols.stop - cols.start), BF)] * len(shifts),
            [VM] * 2 + [ANY],
            2 * len(shifts) * caps * rows_here * width,
            2 * rows_here * width,
        )(rows, features, after)

    def join(*blocks, starts=None, after=()):
        starts = starts or [0] * len(blocks)
        total = sum(b.shape[0] - s for b, s in zip(blocks, starts))
        return call(
            functools.partial(join_kernel, starts),
            vec((total, width), BF),
            [VM] * len(blocks) + [ANY] * len(after),
            0,
            4 * total * width,
            limit=4,
        )(*blocks, *after)

    def add(total, blocks, sizes, at, after, weight=1):
        return call(
            functools.partial(sum_kernel, 512, sizes, at),
            vec((rows_here, width), F32),
            [VM] * (2 + len(blocks)) + [ANY],
            weight * 2 * rows_here * width * sum(sizes),
            8 * rows_here * width,
            scratch=[pltpu.VMEM((sum(sizes), width), BF)],
        )(total, counts, *blocks, after)

    own = call(
        functools.partial(own_kernel, 512),
        vec((rows_here, width), F32),
        [VM] * 3 + [ANY],
        2 * rows_here * width * width,
        8 * rows_here * width,
    )(features, w_self, bias.reshape(1, width), counts)
    total = call(
        functools.partial(local_kernel, 512),
        vec((rows_here, width), F32),
        [VM] * 2 + [ANY],
        2 * rows_here * rows_here * width,
        8 * rows_here * width,
    )(features, counts, own)
    odd = rest(other, slice(0, width), total)
    for shift, block in zip(other, odd):
        got[shift] = swap(block, "member", shift)

    evens = [got[s] for s in range(2, peers, 2)]
    hubs = join(hubs, *evens, starts=[0] + [caps] * len(evens), after=[odd[0]])
    lines = [swap(hubs, "group", shift) for shift in range(1, groups)]
    late = rest([last], spans[0], hubs)
    total = add(total, [got[s] for s in early], [caps] * len(early), rows_here, late[0])
    hubs = join(hubs, *lines, after=[total])
    other_hubs = swap(hubs, "member", 1)
    soon, far_odd = other[:-1] if len(other) > 2 else other[:1], other[-1:]
    at = rows_here + caps * order.index(soon[0])
    total = add(total, [got[s] for s in soon], [caps] * len(soon), at, hubs, 16)
    total = add(total, [hubs, other_hubs], [hub_slots // 2] * 2, rows_here + caps * peers, total)
    late += rest([last], spans[1], total)
    late = [swap(block, "member", last) for block in late]
    at = rows_here + caps * order.index(far_odd[0])
    total = add(total, [got[s] for s in far_odd], [caps] * len(far_odd), at, total)

    at = rows_here + caps * order.index(last)
    value = call(
        functools.partial(late_kernel, 512, at, spans[0]),
        vec((rows_here, width), F32),
        [VM] * 6,
        2 * rows_here * spans[0].stop * width,
        8 * rows_here * width,
    )(own, total, counts, degrees, w_neigh, late[0])
    return call(
        functools.partial(last_kernel, 256, at, spans[1]),
        vec((rows_here, width), BF),
        [VM] * 6,
        2 * rows_here * (width - spans[1].start) * width,
        8 * rows_here * width,
        scratch=[pltpu.VMEM((rows_here, width), BF), pltpu.SemaphoreType.DMA((rows_here // 256,))],
        out_specs=ANY,
    )(value, total, counts, degrees, w_neigh, late[1])


def solution(mesh):
    both = ("group", "member")
    in_specs = (
        P(both, None),
        P(),
        P(),
        P(),
        P(both),
        P(both, None),
        P(both, None),
        P(both, None),
        P(None, both),
        P(both, None, None),
    )
    return jax.shard_map(
        functools.partial(per_device, mesh.shape["group"]),
        mesh=mesh,
        in_specs=in_specs,
        out_specs=P(both, None),
        check_vma=False,
    )
```

```python
import functools

import jax
import jax.numpy as jnp
from jax import lax
from jax.experimental import pallas as pl
from jax.experimental.pallas import tpu as pltpu
from jax.sharding import PartitionSpec as P

LANES = 128
HUB_PAD = 8
CHUNKS = 4
VM = pl.BlockSpec(memory_space=pltpu.VMEM)
ANY = pl.BlockSpec(memory_space=pl.ANY)
HBM = pl.BlockSpec(memory_space=pltpu.HBM)
BF, F32, I32 = jnp.bfloat16, jnp.float32, jnp.int32
vec = jax.ShapeDtypeStruct


def call(kernel, out_shape, in_specs, flops, bytes_accessed, limit=16, scratch=(), out_specs=None):
    single = not isinstance(out_shape, (list, tuple))
    return pl.pallas_call(
        kernel,
        out_shape=out_shape,
        in_specs=in_specs,
        out_specs=out_specs or (VM if single else [VM] * len(out_shape)),
        scratch_shapes=list(scratch),
        compiler_params=pltpu.CompilerParams(vmem_limit_bytes=limit << 20),
        cost_estimate=pl.CostEstimate(flops=4 * flops, bytes_accessed=bytes_accessed, transcendentals=0),
    )


def column_of(row, rows):
    return jnp.transpose(jnp.broadcast_to(row, (8, rows)))[:, :1]


def pick_matrix(rows_ref, shift, rows_here):
    me = lax.axis_index("member")
    caps = rows_ref.shape[1]
    wanted = column_of(rows_ref[pl.ds(me ^ shift, 1), :], caps)
    row_at = lax.broadcasted_iota(I32, (caps, rows_here), 1)
    return jnp.where(row_at == wanted, 1.0, 0.0).astype(BF)


def hub_matrix(hub_ref, rows_here):
    row_at = lax.broadcasted_iota(I32, (HUB_PAD, rows_here), 1)
    line = lax.broadcasted_iota(I32, (HUB_PAD, rows_here), 0)
    hit = jnp.zeros((HUB_PAD, rows_here), F32)
    for h in range(hub_ref.shape[0]):
        hit = hit + jnp.where((line == h) & (row_at == hub_ref[h]), 1.0, 0.0)
    return hit.astype(BF)


def load(small, feat_hbm, feat_ref, sems):
    copies = [pltpu.make_async_copy(a, b, sems.at[n]) for n, (a, b) in enumerate(small)]
    part = feat_ref.shape[0] // CHUNKS
    large = []
    for c in range(CHUNKS):
        span = pl.ds(c * part, part)
        large.append(pltpu.make_async_copy(feat_hbm.at[span, :], feat_ref.at[span, :], sems.at[len(small) + c]))
    for copy in copies + large:
        copy.start()
    for copy in copies:
        copy.wait()
    return large


def picked_rows(picks, feat_ref, copies):
    picks = jnp.concatenate(picks, axis=0)
    part = feat_ref.shape[0] // len(copies)
    picked = None
    for c, copy in enumerate(copies):
        copy.wait()
        span = slice(c * part, (c + 1) * part)
        term = jnp.dot(picks[:, span], feat_ref[span, :], preferred_element_type=F32)
        picked = term if picked is None else picked + term
    return picked.astype(BF)


def first_kernel(shifts, rows_hbm, hub_hbm, feat_hbm, *refs):
    outs, hub_out = refs[: len(shifts)], refs[len(shifts)]
    rows_ref, hub_ref, feat_ref, sems = refs[len(shifts) + 1 :]
    large = load([(rows_hbm, rows_ref), (hub_hbm, hub_ref)], feat_hbm, feat_ref, sems)
    rows_here = feat_ref.shape[0]
    caps = rows_ref.shape[1]
    picks = [pick_matrix(rows_ref, shift, rows_here) for shift in shifts]
    picked = picked_rows(picks + [hub_matrix(hub_ref, rows_here)], feat_ref, large)
    hubs = picked[len(shifts) * caps :]
    hub_out[...] = hubs
    for n in range(len(shifts)):
        block = picked[n * caps : (n + 1) * caps]
        outs[n][...] = jnp.concatenate([block, hubs], axis=0) if shifts[n] % 2 == 0 else block


def near_kernel(shifts, rows_hbm, hub_hbm, feat_hbm, after_ref, *refs):
    outs = refs[: len(shifts)]
    rows_ref, hub_ref, feat_ref, sems = refs[len(shifts) :]
    large = load([(rows_hbm, rows_ref), (hub_hbm, hub_ref)], feat_hbm, feat_ref, sems)
    caps = rows_ref.shape[1]
    picked = picked_rows([pick_matrix(rows_ref, shift, feat_ref.shape[0]) for shift in shifts], feat_ref, large)
    for n, shift in enumerate(shifts):
        block = picked[n * caps : (n + 1) * caps]
        outs[n][...] = jnp.concatenate([block, hub_ref[...]], axis=0) if shift and shift % 2 == 0 else block


def rest_kernel(shifts, cols, rows_ref, feat_ref, after_ref, *outs):
    caps = rows_ref.shape[1]
    picks = [pick_matrix(rows_ref, shift, feat_ref.shape[0]) for shift in shifts]
    picked = jnp.dot(jnp.concatenate(picks, axis=0), feat_ref[:, cols], preferred_element_type=F32).astype(BF)
    for n in range(len(shifts)):
        outs[n][...] = picked[n * caps : (n + 1) * caps]


def join_kernel(starts, *refs):
    out_ref = refs[-1]
    at = 0
    for start, ref in zip(starts, refs):
        size = ref.shape[0] - start
        out_ref[at : at + size, :] = ref[start:, :]
        at += size


def add_counts(index, width, out_ref, row, column):
    rb, kmax = index.shape
    index = index.astype(jnp.int16)
    columns = [jnp.broadcast_to(index[:, k : k + 1], (rb, LANES)) for k in range(kmax)]
    lane = lax.broadcasted_iota(I32, (rb, LANES), 1).astype(jnp.int16)
    one = jnp.ones((rb, LANES), BF)
    zero = jnp.zeros((rb, LANES), BF)
    for g in range(width // LANES):
        number = lane + jnp.asarray(g * LANES, jnp.int16)
        total = zero
        for k in range(kmax):
            total = total + jnp.where(columns[k] == number, one, zero)
        out_ref[pl.ds(row, rb), column + g * LANES : column + (g + 1) * LANES] = total


def table_kernel(rb, peers, caps, hub_dev, magic, order, local_ref, hub_ref, halo_ref, deg_ref, after_ref, out_ref):
    me = lax.axis_index("member")
    group = lax.axis_index("group")
    rows_here = local_ref.shape[1]
    halo_slots = peers * caps
    hub_slots = out_ref.shape[1] - rows_here - halo_slots
    half = peers // 2

    def body(i, carry):
        row = pl.multiple_of(i * rb, rb)
        span = pl.ds(row, rb)

        def masked(which, index):
            slot = lax.broadcasted_iota(I32, index.shape, 0)
            return jnp.transpose(jnp.where(slot < deg_ref[which : which + 1, span], index, -1))

        local = masked(0, local_ref[:, span])
        hub = hub_ref[:, span]
        owner = (hub * magic) >> 16
        apart = (owner & (peers - 1)) ^ me
        line = (owner >> (peers.bit_length() - 1)) ^ group
        place = (apart & 1) * (hub_slots // (2 * HUB_PAD)) + line * half + (apart >> 1)
        hub = masked(1, place * HUB_PAD + hub - owner * hub_dev)
        slot = halo_ref[:, span]
        apart = (slot >> (caps.bit_length() - 1)) ^ me
        place = apart
        for n, shift in enumerate(order):
            if n != shift:
                place = jnp.where(apart == shift, n, place)
        halo = masked(2, place * caps + (slot & (caps - 1)))
        add_counts(local, rows_here, out_ref, row, 0)
        add_counts(halo, halo_slots, out_ref, row, rows_here)
        add_counts(hub, hub_slots, out_ref, row, rows_here + halo_slots)
        return carry

    lax.fori_loop(0, rows_here // rb, body, 0)


def own_kernel(rb, feat_ref, w_ref, bias_ref, after_ref, out_ref):
    bias = bias_ref[...].astype(F32)
    for i in range(feat_ref.shape[0] // rb):
        span = pl.ds(i * rb, rb)
        out_ref[span, :] = jnp.dot(feat_ref[span, :], w_ref[...], preferred_element_type=F32) + bias


def local_kernel(rb, feat_ref, count_ref, after_ref, out_ref):
    rows_here = feat_ref.shape[0]
    for i in range(rows_here // rb):
        span = pl.ds(i * rb, rb)
        out_ref[span, :] = jnp.dot(count_ref[span, :rows_here], feat_ref[...], preferred_element_type=F32)


def sum_kernel(rb, sizes, at, sum_ref, count_ref, *refs):
    blocks, (_, out_ref, joined) = refs[: len(sizes)], refs[len(sizes) :]
    row = 0
    for size, ref in zip(sizes, blocks):
        joined[row : row + size, :] = ref[:size, :]
        row += size
    for i in range(sum_ref.shape[0] // rb):
        span = pl.ds(i * rb, rb)
        out_ref[span, :] = sum_ref[span, :] + jnp.dot(
            count_ref[span, at : at + row], joined[...], preferred_element_type=F32
        )


def mean_part(span, at, cols, sum_ref, count_ref, deg_ref, w_ref, block_ref, value):
    deg = deg_ref[0:1, span] + deg_ref[1:2, span] + deg_ref[2:3, span]
    scale = column_of(1.0 / deg.astype(F32), deg.shape[1])
    counts = count_ref[span, at : at + block_ref.shape[0]]
    total = sum_ref[span, cols] + jnp.dot(counts, block_ref[...], preferred_element_type=F32)
    mean = (total * scale).astype(BF)
    return value + jnp.dot(mean, w_ref[cols, :], preferred_element_type=F32)


def late_kernel(rb, at, cols, own_ref, sum_ref, count_ref, deg_ref, w_ref, block_ref, out_ref):
    for i in range(sum_ref.shape[0] // rb):
        span = pl.ds(i * rb, rb)
        out_ref[span, :] = mean_part(span, at, cols, sum_ref, count_ref, deg_ref, w_ref, block_ref, own_ref[span, :])


def last_kernel(rb, at, cols, own_ref, sum_ref, count_ref, deg_ref, w_ref, block_ref, out_hbm, out_ref, sems):
    copies = []
    for i in range(sum_ref.shape[0] // rb):
        span = pl.ds(i * rb, rb)
        value = mean_part(span, at, cols, sum_ref, count_ref, deg_ref, w_ref, block_ref, own_ref[span, :])
        out_ref[span, :] = jnp.maximum(value, 0.0).astype(BF)
        copies.append(pltpu.make_async_copy(out_ref.at[span, :], out_hbm.at[span, :], sems.at[i]))
        copies[-1].start()
    for copy in copies:
        copy.wait()


def per_device(groups, features, w_self, w_neigh, bias, hub_rows, hub_nbrs, local_nbrs, halo_nbrs, degrees, send_rows):
    rows_here, width = features.shape
    peers, caps = send_rows.shape[1:]
    hub_dev = hub_rows.shape[0]
    magic = -(-(1 << 16) // hub_dev)
    assert all((h * magic) >> 16 == h // hub_dev for h in range(hub_dev * peers * groups))
    assert peers >= 8 and groups >= 4 and hub_dev <= HUB_PAD
    assert not any(n & (n - 1) for n in (peers, groups, caps))
    rows = send_rows.reshape(peers, caps)
    hub_slots = HUB_PAD * peers * groups

    top, last = peers // 2, peers - 1
    far = [last - 1]
    near = list(range(top, last - 1, 2)) + list(range(2, top, 2))
    other = list(range(3, last, 2))
    early = [0, 1] + near + far
    order = early + [last] + other
    spans = [slice(0, width // 2), slice(width // 2, width)]

    def swap(block, axis, shift):
        size = peers if axis == "member" else groups
        return lax.ppermute(block, axis, [(i, i ^ shift) for i in range(size)])

    scratch = [pltpu.VMEM((rows_here, width), BF), pltpu.SemaphoreType.DMA((2 + CHUNKS,))]
    plain, carrier = vec((caps, width), BF), vec((caps + HUB_PAD, width), BF)
    firsts = call(
        functools.partial(first_kernel, far + [1]),
        [carrier] * len(far) + [plain, vec((HUB_PAD, width), BF)],
        [HBM] * 3,
        0,
        2 * rows_here * width,
        limit=60,
        scratch=[pltpu.VMEM((peers, caps), I32), pltpu.SMEM((hub_dev,), I32)] + scratch,
    )(rows, hub_rows, features)
    hubs = firsts[-1]
    got = {shift: swap(block, "member", shift) for shift, block in zip(far + [1], firsts)}
    nears = call(
        functools.partial(near_kernel, near + [0]),
        [plain if shift % 2 else carrier for shift in near] + [plain],
        [HBM] * 3 + [ANY],
        0,
        2 * rows_here * width,
        limit=60,
        scratch=[pltpu.VMEM((peers, caps), I32), pltpu.VMEM((HUB_PAD, width), BF)] + scratch,
    )(rows, hubs, features, got[1])
    for shift, block in zip(near, nears):
        got[shift] = swap(block, "member", shift)
    got[0] = nears[-1]

    counts = call(
        functools.partial(table_kernel, 2 * LANES, peers, caps, hub_dev, magic, order),
        vec((rows_here, rows_here + peers * caps + hub_slots), BF),
        [VM] * 4 + [ANY],
        24 * rows_here * (rows_here + peers * caps),
        2 * rows_here * (rows_here + hub_slots + peers * caps),
    )(local_nbrs.T, hub_nbrs.T, halo_nbrs.T, degrees, got[0])

    def rest(shifts, cols, after):
        return call(
            functools.partial(rest_kernel, shifts, cols),
            [vec((caps, cols.stop - cols.start), BF)] * len(shifts),
            [VM] * 2 + [ANY],
            2 * len(shifts) * caps * rows_here * width,
            2 * rows_here * width,
        )(rows, features, after)

    def join(*blocks, starts=None, after=()):
        starts = starts or [0] * len(blocks)
        total = sum(b.shape[0] - s for b, s in zip(blocks, starts))
        return call(
            functools.partial(join_kernel, starts),
            vec((total, width), BF),
            [VM] * len(blocks) + [ANY] * len(after),
            0,
            4 * total * width,
            limit=4,
        )(*blocks, *after)

    def add(total, blocks, sizes, at, after, weight=1):
        return call(
            functools.partial(sum_kernel, 512, sizes, at),
            vec((rows_here, width), F32),
            [VM] * (2 + len(blocks)) + [ANY],
            weight * 2 * rows_here * width * sum(sizes),
            8 * rows_here * width,
            scratch=[pltpu.VMEM((sum(sizes), width), BF)],
        )(total, counts, *blocks, after)

    own = call(
        functools.partial(own_kernel, 512),
        vec((rows_here, width), F32),
        [VM] * 3 + [ANY],
        2 * rows_here * width * width,
        8 * rows_here * width,
    )(features, w_self, bias.reshape(1, width), counts)
    total = call(
        functools.partial(local_kernel, 512),
        vec((rows_here, width), F32),
        [VM] * 2 + [ANY],
        2 * rows_here * rows_here * width,
        8 * rows_here * width,
    )(features, counts, own)
    odd = rest(other, slice(0, width), total)
    for shift, block in zip(other, odd):
        got[shift] = swap(block, "member", shift)

    evens = [got[s] for s in range(2, peers, 2)]
    hubs = join(hubs, *evens, starts=[0] + [caps] * len(evens), after=[odd[0]])
    lines = [swap(hubs, "group", shift) for shift in range(1, groups)]
    late = rest([last], spans[0], hubs)
    total = add(total, [got[s] for s in early], [caps] * len(early), rows_here, late[0])
    hubs = join(hubs, *lines, after=[total])
    other_hubs = swap(hubs, "member", 1)
    soon, far_odd = other[:-1] if len(other) > 2 else other[:1], other[-1:]
    at = rows_here + caps * order.index(soon[0])
    total = add(total, [got[s] for s in soon], [caps] * len(soon), at, hubs, 16)
    total = add(total, [hubs, other_hubs], [hub_slots // 2] * 2, rows_here + caps * peers, total)
    late += rest([last], spans[1], total)
    late = [swap(block, "member", last) for block in late]
    at = rows_here + caps * order.index(far_odd[0])
    total = add(total, [got[s] for s in far_odd], [caps] * len(far_odd), at, total)

    at = rows_here + caps * order.index(last)
    value = call(
        functools.partial(late_kernel, 512, at, spans[0]),
        vec((rows_here, width), F32),
        [VM] * 6,
        2 * rows_here * spans[0].stop * width,
        8 * rows_here * width,
    )(own, total, counts, degrees, w_neigh, late[0])
    return call(
        functools.partial(last_kernel, 256, at, spans[1]),
        vec((rows_here, width), BF),
        [VM] * 6,
        2 * rows_here * (width - spans[1].start) * width,
        8 * rows_here * width,
        scratch=[pltpu.VMEM((rows_here, width), BF), pltpu.SemaphoreType.DMA((rows_here // 256,))],
        out_specs=ANY,
    )(value, total, counts, degrees, w_neigh, late[1])


def solution(mesh):
    both = ("group", "member")
    in_specs = (
        P(both, None),
        P(),
        P(),
        P(),
        P(both),
        P(both, None),
        P(both, None),
        P(both, None),
        P(None, both),
        P(both, None, None),
    )
    return jax.shard_map(
        functools.partial(per_device, mesh.shape["group"]),
        mesh=mesh,
        in_specs=in_specs,
        out_specs=P(both, None),
        check_vma=False,
    )
```

```python
import functools

import jax
import jax.numpy as jnp
from jax import lax
from jax.experimental import pallas as pl
from jax.experimental.pallas import tpu as pltpu
from jax.sharding import PartitionSpec as P

LANES = 128
HUB_PAD = 8
HUB_COPY = 16
CHUNKS = 4
VM = pl.BlockSpec(memory_space=pltpu.VMEM)
ANY = pl.BlockSpec(memory_space=pl.ANY)
HBM = pl.BlockSpec(memory_space=pltpu.HBM)
BF, F32, I32 = jnp.bfloat16, jnp.float32, jnp.int32
vec = jax.ShapeDtypeStruct


def call(kernel, out_shape, in_specs, flops, bytes_accessed, limit=16, scratch=(), out_specs=None):
    single = not isinstance(out_shape, (list, tuple))
    return pl.pallas_call(
        kernel,
        out_shape=out_shape,
        in_specs=in_specs,
        out_specs=out_specs or (VM if single else [VM] * len(out_shape)),
        scratch_shapes=list(scratch),
        compiler_params=pltpu.CompilerParams(vmem_limit_bytes=limit << 20),
        cost_estimate=pl.CostEstimate(flops=4 * flops, bytes_accessed=bytes_accessed, transcendentals=0),
    )


def column_of(row, rows):
    return jnp.transpose(jnp.broadcast_to(row, (8, rows)))[:, :1]


def pick_matrix(rows_ref, shift, rows_here):
    me = lax.axis_index("member")
    caps = rows_ref.shape[1]
    wanted = column_of(rows_ref[pl.ds(me ^ shift, 1), :], caps)
    row_at = lax.broadcasted_iota(I32, (caps, rows_here), 1)
    return jnp.where(row_at == wanted, 1.0, 0.0).astype(BF)


def hub_matrix(hub_ref, rows_here):
    row_at = lax.broadcasted_iota(I32, (HUB_COPY, rows_here), 1)
    line = lax.broadcasted_iota(I32, (HUB_COPY, rows_here), 0)
    hit = jnp.zeros((HUB_COPY, rows_here), F32)
    for h in range(hub_ref.shape[0]):
        hit = hit + jnp.where((line == h) & (row_at == hub_ref[h]), 1.0, 0.0)
    return hit.astype(BF)


def load(small, feat_hbm, feat_ref, sems):
    copies = [pltpu.make_async_copy(a, b, sems.at[n]) for n, (a, b) in enumerate(small)]
    part = feat_ref.shape[0] // CHUNKS
    large = []
    for c in range(CHUNKS):
        span = pl.ds(c * part, part)
        large.append(pltpu.make_async_copy(feat_hbm.at[span, :], feat_ref.at[span, :], sems.at[len(small) + c]))
    for copy in copies + large:
        copy.start()
    for copy in copies:
        copy.wait()
    return large


def picked_rows(picks, feat_ref, copies):
    picks = jnp.concatenate(picks, axis=0)
    part = feat_ref.shape[0] // len(copies)
    picked = None
    for c, copy in enumerate(copies):
        copy.wait()
        span = slice(c * part, (c + 1) * part)
        term = jnp.dot(picks[:, span], feat_ref[span, :], preferred_element_type=F32)
        picked = term if picked is None else picked + term
    return picked.astype(BF)


def first_kernel(shifts, rows_hbm, hub_hbm, feat_hbm, *refs):
    outs, hub_out = refs[: len(shifts)], refs[len(shifts)]
    rows_ref, hub_ref, feat_ref, sems = refs[len(shifts) + 1 :]
    large = load([(rows_hbm, rows_ref), (hub_hbm, hub_ref)], feat_hbm, feat_ref, sems)
    rows_here = feat_ref.shape[0]
    caps = rows_ref.shape[1]
    picks = [pick_matrix(rows_ref, shift, rows_here) for shift in shifts]
    picked = picked_rows(picks + [hub_matrix(hub_ref, rows_here)], feat_ref, large)
    hubs = picked[len(shifts) * caps :]
    hub_out[...] = hubs
    for n in range(len(shifts)):
        block = picked[n * caps : (n + 1) * caps]
        outs[n][...] = jnp.concatenate([block, hubs[:HUB_PAD]], axis=0) if shifts[n] % 2 == 0 else block


def near_kernel(shifts, rows_hbm, hub_hbm, feat_hbm, after_ref, *refs):
    outs = refs[: len(shifts)]
    rows_ref, hub_ref, feat_ref, sems = refs[len(shifts) :]
    large = load([(rows_hbm, rows_ref), (hub_hbm, hub_ref)], feat_hbm, feat_ref, sems)
    caps = rows_ref.shape[1]
    picked = picked_rows([pick_matrix(rows_ref, shift, feat_ref.shape[0]) for shift in shifts], feat_ref, large)
    for n, shift in enumerate(shifts):
        block = picked[n * caps : (n + 1) * caps]
        outs[n][...] = jnp.concatenate([block, hub_ref[...][:HUB_PAD]], axis=0) if shift and shift % 2 == 0 else block


def rest_kernel(shifts, cols, rows_ref, feat_ref, after_ref, *outs):
    caps = rows_ref.shape[1]
    picks = [pick_matrix(rows_ref, shift, feat_ref.shape[0]) for shift in shifts]
    picked = jnp.dot(jnp.concatenate(picks, axis=0), feat_ref[:, cols], preferred_element_type=F32).astype(BF)
    for n in range(len(shifts)):
        outs[n][...] = picked[n * caps : (n + 1) * caps]


def join_kernel(spans, *refs):
    out_ref = refs[-1]
    at = 0
    for (start, stop), ref in zip(spans, refs):
        out_ref[at : at + stop - start, :] = ref[start:stop, :]
        at += stop - start


def add_counts(index, width, out_ref, row, column):
    rb, kmax = index.shape
    index = index.astype(jnp.int16)
    columns = [jnp.broadcast_to(index[:, k : k + 1], (rb, LANES)) for k in range(kmax)]
    lane = lax.broadcasted_iota(I32, (rb, LANES), 1).astype(jnp.int16)
    one = jnp.ones((rb, LANES), BF)
    zero = jnp.zeros((rb, LANES), BF)
    for g in range(width // LANES):
        number = lane + jnp.asarray(g * LANES, jnp.int16)
        total = zero
        for k in range(kmax):
            total = total + jnp.where(columns[k] == number, one, zero)
        out_ref[pl.ds(row, rb), column + g * LANES : column + (g + 1) * LANES] = total


def table_kernel(rb, peers, caps, hub_dev, magic, order, local_ref, hub_ref, halo_ref, deg_ref, after_ref, out_ref):
    me = lax.axis_index("member")
    group = lax.axis_index("group")
    rows_here = local_ref.shape[1]
    halo_slots = peers * caps
    hub_slots = out_ref.shape[1] - rows_here - halo_slots
    half = peers // 2

    def body(i, carry):
        row = pl.multiple_of(i * rb, rb)
        span = pl.ds(row, rb)

        def masked(which, index):
            slot = lax.broadcasted_iota(I32, index.shape, 0)
            return jnp.transpose(jnp.where(slot < deg_ref[which : which + 1, span], index, -1))

        local = masked(0, local_ref[:, span])
        hub = hub_ref[:, span]
        owner = (hub * magic) >> 16
        apart = (owner & (peers - 1)) ^ me
        line = (owner >> (peers.bit_length() - 1)) ^ group
        place = (apart & 1) * (hub_slots // (2 * HUB_PAD)) + line * half + (apart >> 1)
        hub = masked(1, place * HUB_PAD + hub - owner * hub_dev)
        slot = halo_ref[:, span]
        apart = (slot >> (caps.bit_length() - 1)) ^ me
        place = apart
        for n, shift in enumerate(order):
            if n != shift:
                place = jnp.where(apart == shift, n, place)
        halo = masked(2, place * caps + (slot & (caps - 1)))
        add_counts(local, rows_here, out_ref, row, 0)
        add_counts(halo, halo_slots, out_ref, row, rows_here)
        add_counts(hub, hub_slots, out_ref, row, rows_here + halo_slots)
        return carry

    lax.fori_loop(0, rows_here // rb, body, 0)


def own_kernel(rb, feat_ref, w_ref, bias_ref, after_ref, out_ref):
    bias = bias_ref[...].astype(F32)
    for i in range(feat_ref.shape[0] // rb):
        span = pl.ds(i * rb, rb)
        out_ref[span, :] = jnp.dot(feat_ref[span, :], w_ref[...], preferred_element_type=F32) + bias


def local_kernel(rb, feat_ref, count_ref, after_ref, out_ref):
    rows_here = feat_ref.shape[0]
    for i in range(rows_here // rb):
        span = pl.ds(i * rb, rb)
        out_ref[span, :] = jnp.dot(count_ref[span, :rows_here], feat_ref[...], preferred_element_type=F32)


def sum_kernel(rb, sizes, at, sum_ref, count_ref, *refs):
    blocks, (_, out_ref, joined) = refs[: len(sizes)], refs[len(sizes) :]
    row = 0
    for size, ref in zip(sizes, blocks):
        joined[row : row + size, :] = ref[:size, :]
        row += size
    for i in range(sum_ref.shape[0] // rb):
        span = pl.ds(i * rb, rb)
        out_ref[span, :] = sum_ref[span, :] + jnp.dot(
            count_ref[span, at : at + row], joined[...], preferred_element_type=F32
        )


def means(at, cols, sum_ref, count_ref, deg_ref, block_ref, mean_ref):
    rb = 512
    for i in range(sum_ref.shape[0] // rb):
        span = pl.ds(i * rb, rb)
        deg = deg_ref[0:1, span] + deg_ref[1:2, span] + deg_ref[2:3, span]
        scale = column_of(1.0 / deg.astype(F32), rb)
        counts = count_ref[span, at : at + block_ref.shape[0]]
        total = sum_ref[span, cols] + jnp.dot(counts, block_ref[...], preferred_element_type=F32)
        mean_ref[span, :] = (total * scale).astype(BF)


def late_kernel(rb, at, cols, own_ref, sum_ref, count_ref, deg_ref, w_ref, block_ref, out_ref, mean_ref):
    means(at, cols, sum_ref, count_ref, deg_ref, block_ref, mean_ref)
    for i in range(sum_ref.shape[0] // rb):
        span = pl.ds(i * rb, rb)
        out_ref[span, :] = own_ref[span, :] + jnp.dot(mean_ref[span, :], w_ref[cols, :], preferred_element_type=F32)


def last_kernel(rb, at, cols, own_ref, sum_ref, count_ref, deg_ref, w_ref, block_ref, out_hbm, mean_ref, out_ref, sems):
    means(at, cols, sum_ref, count_ref, deg_ref, block_ref, mean_ref)
    copies = []
    for i in range(sum_ref.shape[0] // rb):
        span = pl.ds(i * rb, rb)
        value = own_ref[span, :] + jnp.dot(mean_ref[span, :], w_ref[cols, :], preferred_element_type=F32)
        out_ref[span, :] = jnp.maximum(value, 0.0).astype(BF)
        copies.append(pltpu.make_async_copy(out_ref.at[span, :], out_hbm.at[span, :], sems.at[i]))
        copies[-1].start()
    for copy in copies:
        copy.wait()


def per_device(groups, features, w_self, w_neigh, bias, hub_rows, hub_nbrs, local_nbrs, halo_nbrs, degrees, send_rows):
    rows_here, width = features.shape
    peers, caps = send_rows.shape[1:]
    hub_dev = hub_rows.shape[0]
    magic = -(-(1 << 16) // hub_dev)
    assert all((h * magic) >> 16 == h // hub_dev for h in range(hub_dev * peers * groups))
    assert peers >= 8 and groups >= 4 and hub_dev <= HUB_PAD
    assert not any(n & (n - 1) for n in (peers, groups, caps))
    rows = send_rows.reshape(peers, caps)
    hub_slots = HUB_PAD * peers * groups

    top, last = peers // 2, peers - 1
    far = [last - 1]
    near = list(range(top, last - 1, 2)) + list(range(2, top, 2))
    other = list(range(3, last, 2))
    early = [0, 1] + near + far
    order = early + [last] + other
    spans = [slice(0, width // 2), slice(width // 2, width)]

    def swap(block, axis, shift):
        size = peers if axis == "member" else groups
        return lax.ppermute(block, axis, [(i, i ^ shift) for i in range(size)])

    scratch = [pltpu.VMEM((rows_here, width), BF), pltpu.SemaphoreType.DMA((2 + CHUNKS,))]
    plain, carrier = vec((caps, width), BF), vec((caps + HUB_PAD, width), BF)
    firsts = call(
        functools.partial(first_kernel, far + [1]),
        [carrier] * len(far) + [plain, vec((HUB_COPY, width), BF)],
        [HBM] * 3,
        0,
        2 * rows_here * width,
        limit=60,
        scratch=[pltpu.VMEM((peers, caps), I32), pltpu.SMEM((hub_dev,), I32)] + scratch,
    )(rows, hub_rows, features)
    hubs = firsts[-1]
    got = {shift: swap(block, "member", shift) for shift, block in zip(far + [1], firsts)}
    nears = call(
        functools.partial(near_kernel, near + [0]),
        [plain if shift % 2 else carrier for shift in near] + [plain],
        [HBM] * 3 + [ANY],
        0,
        2 * rows_here * width,
        limit=60,
        scratch=[pltpu.VMEM((peers, caps), I32), pltpu.VMEM((HUB_COPY, width), BF)] + scratch,
    )(rows, hubs, features, got[1])
    for shift, block in zip(near, nears):
        got[shift] = swap(block, "member", shift)
    got[0] = nears[-1]

    counts = call(
        functools.partial(table_kernel, 2 * LANES, peers, caps, hub_dev, magic, order),
        vec((rows_here, rows_here + peers * caps + hub_slots), BF),
        [VM] * 4 + [ANY],
        24 * rows_here * (rows_here + peers * caps),
        2 * rows_here * (rows_here + hub_slots + peers * caps),
    )(local_nbrs.T, hub_nbrs.T, halo_nbrs.T, degrees, got[0])

    def rest(shifts, cols, after, weight=1):
        return call(
            functools.partial(rest_kernel, shifts, cols),
            [vec((caps, cols.stop - cols.start), BF)] * len(shifts),
            [VM] * 2 + [ANY],
            weight * 2 * len(shifts) * caps * rows_here * width,
            2 * rows_here * width,
        )(rows, features, after)

    def join(blocks, spans, after):
        total = sum(stop - start for start, stop in spans)
        return call(
            functools.partial(join_kernel, spans),
            vec((total, width), BF),
            [VM] * len(blocks) + [ANY],
            0,
            4 * total * width,
            limit=4,
        )(*blocks, after)

    def add(total, blocks, sizes, at, after, weight=1):
        return call(
            functools.partial(sum_kernel, 512, sizes, at),
            vec((rows_here, width), F32),
            [VM] * (2 + len(blocks)) + [ANY],
            weight * 2 * rows_here * width * sum(sizes),
            8 * rows_here * width,
            scratch=[pltpu.VMEM((sum(sizes), width), BF)],
        )(total, counts, *blocks, after)

    own = call(
        functools.partial(own_kernel, 512),
        vec((rows_here, width), F32),
        [VM] * 3 + [ANY],
        2 * rows_here * width * width,
        8 * rows_here * width,
    )(features, w_self, bias.reshape(1, width), counts)
    total = call(
        functools.partial(local_kernel, 512),
        vec((rows_here, width), F32),
        [VM] * 2 + [ANY],
        2 * rows_here * rows_here * width,
        8 * rows_here * width,
    )(features, counts, own)
    odd = rest(other, slice(0, width), total)
    for shift, block in zip(other, odd):
        got[shift] = swap(block, "member", shift)

    evens = [got[s] for s in range(2, peers, 2)]
    hubs = join([hubs, *evens], [(0, HUB_PAD)] + [(caps, caps + HUB_PAD)] * len(evens), odd[0])
    lines = [swap(hubs, "group", shift) for shift in range(1, groups)]
    late = rest([last], spans[0], hubs, 32)
    hubs = join([hubs, *lines], [(0, hubs.shape[0])] * groups, late[0])
    other_hubs = swap(hubs, "member", 1)
    total = add(total, [got[s] for s in early], [caps] * len(early), rows_here, hubs, 16)
    total = add(total, [hubs, other_hubs], [hub_slots // 2] * 2, rows_here + caps * peers, total)
    late += rest([last], spans[1], total)
    late = [swap(block, "member", last) for block in late]
    at = rows_here + caps * order.index(other[0])
    total = add(total, [got[s] for s in other], [caps] * len(other), at, total)

    at = rows_here + caps * order.index(last)
    value = call(
        functools.partial(late_kernel, 512, at, spans[0]),
        vec((rows_here, width), F32),
        [VM] * 6,
        2 * rows_here * spans[0].stop * width,
        8 * rows_here * width,
        scratch=[pltpu.VMEM((rows_here, spans[0].stop), BF)],
    )(own, total, counts, degrees, w_neigh, late[0])
    return call(
        functools.partial(last_kernel, 256, at, spans[1]),
        vec((rows_here, width), BF),
        [VM] * 6,
        2 * rows_here * (width - spans[1].start) * width,
        8 * rows_here * width,
        scratch=[
            pltpu.VMEM((rows_here, width - spans[1].start), BF),
            pltpu.VMEM((rows_here, width), BF),
            pltpu.SemaphoreType.DMA((rows_here // 256,)),
        ],
        out_specs=ANY,
    )(value, total, counts, degrees, w_neigh, late[1])


def solution(mesh):
    both = ("group", "member")
    in_specs = (
        P(both, None),
        P(),
        P(),
        P(),
        P(both),
        P(both, None),
        P(both, None),
        P(both, None),
        P(None, both),
        P(both, None, None),
    )
    return jax.shard_map(
        functools.partial(per_device, mesh.shape["group"]),
        mesh=mesh,
        in_specs=in_specs,
        out_specs=P(both, None),
        check_vma=False,
    )
```

```python
import functools

import jax
import jax.numpy as jnp
from jax import lax
from jax.experimental import pallas as pl
from jax.experimental.pallas import tpu as pltpu
from jax.sharding import PartitionSpec as P

LANES = 128
HUB_PAD = 8
HUB_COPY = 16
CHUNKS = 4
VM = pl.BlockSpec(memory_space=pltpu.VMEM)
ANY = pl.BlockSpec(memory_space=pl.ANY)
HBM = pl.BlockSpec(memory_space=pltpu.HBM)
BF, F32, I32 = jnp.bfloat16, jnp.float32, jnp.int32
vec = jax.ShapeDtypeStruct


def call(kernel, out_shape, in_specs, flops, bytes_accessed, limit=16, scratch=(), out_specs=None):
    single = not isinstance(out_shape, (list, tuple))
    return pl.pallas_call(
        kernel,
        out_shape=out_shape,
        in_specs=in_specs,
        out_specs=out_specs or (VM if single else [VM] * len(out_shape)),
        scratch_shapes=list(scratch),
        compiler_params=pltpu.CompilerParams(vmem_limit_bytes=limit << 20),
        cost_estimate=pl.CostEstimate(flops=4 * flops, bytes_accessed=bytes_accessed, transcendentals=0),
    )


def column_of(row, rows):
    return jnp.transpose(jnp.broadcast_to(row, (8, rows)))[:, :1]


def pick_matrix(rows_ref, shift, rows_here):
    me = lax.axis_index("member")
    caps = rows_ref.shape[1]
    wanted = column_of(rows_ref[pl.ds(me ^ shift, 1), :], caps)
    row_at = lax.broadcasted_iota(I32, (caps, rows_here), 1)
    return jnp.where(row_at == wanted, 1.0, 0.0).astype(BF)


def hub_matrix(hub_ref, rows_here):
    row_at = lax.broadcasted_iota(I32, (HUB_COPY, rows_here), 1)
    line = lax.broadcasted_iota(I32, (HUB_COPY, rows_here), 0)
    hit = jnp.zeros((HUB_COPY, rows_here), F32)
    for h in range(hub_ref.shape[0]):
        hit = hit + jnp.where((line == h) & (row_at == hub_ref[h]), 1.0, 0.0)
    return hit.astype(BF)


def load(small, feat_hbm, feat_ref, sems):
    copies = [pltpu.make_async_copy(a, b, sems.at[n]) for n, (a, b) in enumerate(small)]
    part = feat_ref.shape[0] // CHUNKS
    large = []
    for c in range(CHUNKS):
        span = pl.ds(c * part, part)
        large.append(pltpu.make_async_copy(feat_hbm.at[span, :], feat_ref.at[span, :], sems.at[len(small) + c]))
    for copy in copies + large:
        copy.start()
    for copy in copies:
        copy.wait()
    return large


def picked_rows(picks, feat_ref, copies):
    picks = jnp.concatenate(picks, axis=0)
    part = feat_ref.shape[0] // len(copies)
    picked = None
    for c, copy in enumerate(copies):
        copy.wait()
        span = slice(c * part, (c + 1) * part)
        term = jnp.dot(picks[:, span], feat_ref[span, :], preferred_element_type=F32)
        picked = term if picked is None else picked + term
    return picked.astype(BF)


def first_kernel(shifts, rows_hbm, hub_hbm, feat_hbm, *refs):
    outs, hub_out = refs[: len(shifts)], refs[len(shifts)]
    rows_ref, hub_ref, feat_ref, sems = refs[len(shifts) + 1 :]
    large = load([(rows_hbm, rows_ref), (hub_hbm, hub_ref)], feat_hbm, feat_ref, sems)
    rows_here = feat_ref.shape[0]
    caps = rows_ref.shape[1]
    picks = [pick_matrix(rows_ref, shift, rows_here) for shift in shifts]
    picked = picked_rows(picks + [hub_matrix(hub_ref, rows_here)], feat_ref, large)
    hubs = picked[len(shifts) * caps :]
    hub_out[...] = hubs
    for n in range(len(shifts)):
        block = picked[n * caps : (n + 1) * caps]
        outs[n][...] = jnp.concatenate([block, hubs[:HUB_PAD]], axis=0) if shifts[n] % 2 == 0 else block


def near_kernel(shifts, rows_hbm, hub_hbm, feat_hbm, after_ref, *refs):
    outs = refs[: len(shifts)]
    rows_ref, hub_ref, feat_ref, sems = refs[len(shifts) :]
    large = load([(rows_hbm, rows_ref), (hub_hbm, hub_ref)], feat_hbm, feat_ref, sems)
    caps = rows_ref.shape[1]
    picked = picked_rows([pick_matrix(rows_ref, shift, feat_ref.shape[0]) for shift in shifts], feat_ref, large)
    for n, shift in enumerate(shifts):
        block = picked[n * caps : (n + 1) * caps]
        outs[n][...] = jnp.concatenate([block, hub_ref[...][:HUB_PAD]], axis=0) if shift and shift % 2 == 0 else block


def rest_kernel(shifts, cols, rows_ref, feat_ref, after_ref, *outs):
    caps = rows_ref.shape[1]
    picks = [pick_matrix(rows_ref, shift, feat_ref.shape[0]) for shift in shifts]
    picked = jnp.dot(jnp.concatenate(picks, axis=0), feat_ref[:, cols], preferred_element_type=F32).astype(BF)
    for n in range(len(shifts)):
        outs[n][...] = picked[n * caps : (n + 1) * caps]


def join_kernel(spans, *refs):
    out_ref = refs[-1]
    at = 0
    for (start, stop), ref in zip(spans, refs):
        out_ref[at : at + stop - start, :] = ref[start:stop, :]
        at += stop - start


def add_counts(index, width, out_ref, row, column):
    rb, kmax = index.shape
    index = index.astype(jnp.int16)
    columns = [jnp.broadcast_to(index[:, k : k + 1], (rb, LANES)) for k in range(kmax)]
    lane = lax.broadcasted_iota(I32, (rb, LANES), 1).astype(jnp.int16)
    one = jnp.ones((rb, LANES), BF)
    zero = jnp.zeros((rb, LANES), BF)
    for g in range(width // LANES):
        number = lane + jnp.asarray(g * LANES, jnp.int16)
        total = zero
        for k in range(kmax):
            total = total + jnp.where(columns[k] == number, one, zero)
        out_ref[pl.ds(row, rb), column + g * LANES : column + (g + 1) * LANES] = total


def table_kernel(rb, peers, caps, hub_dev, magic, order, local_ref, hub_ref, halo_ref, deg_ref, after_ref, out_ref):
    me = lax.axis_index("member")
    group = lax.axis_index("group")
    rows_here = local_ref.shape[1]
    halo_slots = peers * caps
    hub_slots = out_ref.shape[1] - rows_here - halo_slots
    half = peers // 2

    def body(i, carry):
        row = pl.multiple_of(i * rb, rb)
        span = pl.ds(row, rb)

        def masked(which, index):
            slot = lax.broadcasted_iota(I32, index.shape, 0)
            return jnp.transpose(jnp.where(slot < deg_ref[which : which + 1, span], index, -1))

        local = masked(0, local_ref[:, span])
        hub = hub_ref[:, span]
        owner = (hub * magic) >> 16
        apart = (owner & (peers - 1)) ^ me
        line = (owner >> (peers.bit_length() - 1)) ^ group
        place = (apart & 1) * (hub_slots // (2 * HUB_PAD)) + line * half + (apart >> 1)
        hub = masked(1, place * HUB_PAD + hub - owner * hub_dev)
        slot = halo_ref[:, span]
        apart = (slot >> (caps.bit_length() - 1)) ^ me
        place = apart
        for n, shift in enumerate(order):
            if n != shift:
                place = jnp.where(apart == shift, n, place)
        halo = masked(2, place * caps + (slot & (caps - 1)))
        add_counts(local, rows_here, out_ref, row, 0)
        add_counts(halo, halo_slots, out_ref, row, rows_here)
        add_counts(hub, hub_slots, out_ref, row, rows_here + halo_slots)
        return carry

    lax.fori_loop(0, rows_here // rb, body, 0)


def own_kernel(rb, feat_ref, w_ref, bias_ref, after_ref, out_ref):
    bias = bias_ref[...].astype(F32)
    for i in range(feat_ref.shape[0] // rb):
        span = pl.ds(i * rb, rb)
        out_ref[span, :] = jnp.dot(feat_ref[span, :], w_ref[...], preferred_element_type=F32) + bias


def local_kernel(rb, feat_ref, count_ref, after_ref, out_ref):
    rows_here = feat_ref.shape[0]
    for i in range(rows_here // rb):
        span = pl.ds(i * rb, rb)
        out_ref[span, :] = jnp.dot(count_ref[span, :rows_here], feat_ref[...], preferred_element_type=F32)


def sum_kernel(rb, sizes, at, sum_ref, count_ref, *refs):
    blocks, (_, out_ref, joined) = refs[: len(sizes)], refs[len(sizes) :]
    row = 0
    for size, ref in zip(sizes, blocks):
        joined[row : row + size, :] = ref[:size, :]
        row += size
    for i in range(sum_ref.shape[0] // rb):
        span = pl.ds(i * rb, rb)
        out_ref[span, :] = sum_ref[span, :] + jnp.dot(
            count_ref[span, at : at + row], joined[...], preferred_element_type=F32
        )


def means(at, cols, sum_ref, count_ref, deg_ref, block_ref, mean_ref):
    rb = 512
    for i in range(sum_ref.shape[0] // rb):
        span = pl.ds(i * rb, rb)
        deg = deg_ref[0:1, span] + deg_ref[1:2, span] + deg_ref[2:3, span]
        scale = column_of(1.0 / deg.astype(F32), rb)
        counts = count_ref[span, at : at + block_ref.shape[0]]
        total = sum_ref[span, cols] + jnp.dot(counts, block_ref[...], preferred_element_type=F32)
        mean_ref[span, :] = (total * scale).astype(BF)


def late_kernel(rb, at, cols, own_ref, sum_ref, count_ref, deg_ref, w_ref, block_ref, out_ref, mean_ref):
    means(at, cols, sum_ref, count_ref, deg_ref, block_ref, mean_ref)
    for i in range(sum_ref.shape[0] // rb):
        span = pl.ds(i * rb, rb)
        out_ref[span, :] = own_ref[span, :] + jnp.dot(mean_ref[span, :], w_ref[cols, :], preferred_element_type=F32)


def last_kernel(rb, at, cols, own_ref, sum_ref, count_ref, deg_ref, w_ref, block_ref, out_hbm, mean_ref, out_ref, sems):
    means(at, cols, sum_ref, count_ref, deg_ref, block_ref, mean_ref)
    copies = []
    for i in range(sum_ref.shape[0] // rb):
        span = pl.ds(i * rb, rb)
        value = own_ref[span, :] + jnp.dot(mean_ref[span, :], w_ref[cols, :], preferred_element_type=F32)
        out_ref[span, :] = jnp.maximum(value, 0.0).astype(BF)
        copies.append(pltpu.make_async_copy(out_ref.at[span, :], out_hbm.at[span, :], sems.at[i]))
        copies[-1].start()
    for copy in copies:
        copy.wait()


def per_device(groups, features, w_self, w_neigh, bias, hub_rows, hub_nbrs, local_nbrs, halo_nbrs, degrees, send_rows):
    rows_here, width = features.shape
    peers, caps = send_rows.shape[1:]
    hub_dev = hub_rows.shape[0]
    magic = -(-(1 << 16) // hub_dev)
    assert all((h * magic) >> 16 == h // hub_dev for h in range(hub_dev * peers * groups))
    assert peers >= 8 and groups >= 4 and hub_dev <= HUB_PAD
    assert not any(n & (n - 1) for n in (peers, groups, caps))
    rows = send_rows.reshape(peers, caps)
    hub_slots = HUB_PAD * peers * groups

    top, last = peers // 2, peers - 1
    far = [last - 1]
    near = list(range(top, last - 1, 2)) + list(range(2, top, 2))
    other = list(range(3, last, 2))
    early = [0, 1] + near + far
    order = early + [last] + other
    cuts = [0, width // 2, 3 * width // 4, width]
    spans = [slice(a, b) for a, b in zip(cuts, cuts[1:])]

    def swap(block, axis, shift):
        size = peers if axis == "member" else groups
        return lax.ppermute(block, axis, [(i, i ^ shift) for i in range(size)])

    scratch = [pltpu.VMEM((rows_here, width), BF), pltpu.SemaphoreType.DMA((2 + CHUNKS,))]
    plain, carrier = vec((caps, width), BF), vec((caps + HUB_PAD, width), BF)
    firsts = call(
        functools.partial(first_kernel, far + [1]),
        [carrier] * len(far) + [plain, vec((HUB_COPY, width), BF)],
        [HBM] * 3,
        0,
        2 * rows_here * width,
        limit=60,
        scratch=[pltpu.VMEM((peers, caps), I32), pltpu.SMEM((hub_dev,), I32)] + scratch,
    )(rows, hub_rows, features)
    hubs = firsts[-1]
    got = {shift: swap(block, "member", shift) for shift, block in zip(far + [1], firsts)}
    nears = call(
        functools.partial(near_kernel, near + [0]),
        [plain if shift % 2 else carrier for shift in near] + [plain],
        [HBM] * 3 + [ANY],
        0,
        2 * rows_here * width,
        limit=60,
        scratch=[pltpu.VMEM((peers, caps), I32), pltpu.VMEM((HUB_COPY, width), BF)] + scratch,
    )(rows, hubs, features, got[1])
    for shift, block in zip(near, nears):
        got[shift] = swap(block, "member", shift)
    got[0] = nears[-1]

    counts = call(
        functools.partial(table_kernel, 2 * LANES, peers, caps, hub_dev, magic, order),
        vec((rows_here, rows_here + peers * caps + hub_slots), BF),
        [VM] * 4 + [ANY],
        24 * rows_here * (rows_here + peers * caps),
        2 * rows_here * (rows_here + hub_slots + peers * caps),
    )(local_nbrs.T, hub_nbrs.T, halo_nbrs.T, degrees, got[0])

    def rest(shifts, cols, after, weight=1):
        return call(
            functools.partial(rest_kernel, shifts, cols),
            [vec((caps, cols.stop - cols.start), BF)] * len(shifts),
            [VM] * 2 + [ANY],
            weight * 2 * len(shifts) * caps * rows_here * width,
            2 * rows_here * width,
        )(rows, features, after)

    def join(blocks, spans, after):
        total = sum(stop - start for start, stop in spans)
        return call(
            functools.partial(join_kernel, spans),
            vec((total, width), BF),
            [VM] * len(blocks) + [ANY],
            0,
            4 * total * width,
            limit=4,
        )(*blocks, after)

    def add(total, blocks, sizes, at, after, weight=1):
        return call(
            functools.partial(sum_kernel, 512, sizes, at),
            vec((rows_here, width), F32),
            [VM] * (2 + len(blocks)) + [ANY],
            weight * 2 * rows_here * width * sum(sizes),
            8 * rows_here * width,
            scratch=[pltpu.VMEM((sum(sizes), width), BF)],
        )(total, counts, *blocks, after)

    own = call(
        functools.partial(own_kernel, 512),
        vec((rows_here, width), F32),
        [VM] * 3 + [ANY],
        2 * rows_here * width * width,
        8 * rows_here * width,
    )(features, w_self, bias.reshape(1, width), counts)
    total = call(
        functools.partial(local_kernel, 512),
        vec((rows_here, width), F32),
        [VM] * 2 + [ANY],
        2 * rows_here * rows_here * width,
        8 * rows_here * width,
    )(features, counts, own)
    odd = rest(other, slice(0, width), total)
    for shift, block in zip(other, odd):
        got[shift] = swap(block, "member", shift)

    evens = [got[s] for s in range(2, peers, 2)]
    hubs = join([hubs, *evens], [(0, HUB_PAD)] + [(caps, caps + HUB_PAD)] * len(evens), odd[0])
    lines = [swap(hubs, "group", shift) for shift in range(1, groups)]
    late = rest([last], spans[0], hubs, 32)
    hubs = join([hubs, *lines], [(0, hubs.shape[0])] * groups, late[0])
    other_hubs = swap(hubs, "member", 1)
    total = add(total, [got[s] for s in early], [caps] * len(early), rows_here, hubs, 16)
    total = add(total, [hubs, other_hubs], [hub_slots // 2] * 2, rows_here + caps * peers, total)
    late += rest([last], spans[1], total)
    at = rows_here + caps * order.index(other[0])
    total = add(total, [got[s] for s in other], [caps] * len(other), at, total)
    late += rest([last], spans[2], total)
    late = [swap(block, "member", last) for block in late]

    at = rows_here + caps * order.index(last)
    value = own
    for span, block in zip(spans[:-1], late):
        value = call(
            functools.partial(late_kernel, 512, at, span),
            vec((rows_here, width), F32),
            [VM] * 6,
            2 * rows_here * (span.stop - span.start) * width,
            8 * rows_here * width,
            scratch=[pltpu.VMEM((rows_here, span.stop - span.start), BF)],
        )(value, total, counts, degrees, w_neigh, block)
    return call(
        functools.partial(last_kernel, 256, at, spans[-1]),
        vec((rows_here, width), BF),
        [VM] * 6,
        2 * rows_here * (width - spans[-1].start) * width,
        8 * rows_here * width,
        scratch=[
            pltpu.VMEM((rows_here, width - spans[-1].start), BF),
            pltpu.VMEM((rows_here, width), BF),
            pltpu.SemaphoreType.DMA((rows_here // 256,)),
        ],
        out_specs=ANY,
    )(value, total, counts, degrees, w_neigh, late[-1])


def solution(mesh):
    both = ("group", "member")
    in_specs = (
        P(both, None),
        P(),
        P(),
        P(),
        P(both),
        P(both, None),
        P(both, None),
        P(both, None),
        P(None, both),
        P(both, None, None),
    )
    return jax.shard_map(
        functools.partial(per_device, mesh.shape["group"]),
        mesh=mesh,
        in_specs=in_specs,
        out_specs=P(both, None),
        check_vma=False,
    )
```

```python
import functools

import jax
import jax.numpy as jnp
from jax import lax
from jax.experimental import pallas as pl
from jax.experimental.pallas import tpu as pltpu
from jax.sharding import PartitionSpec as P

LANES = 128
HUB_PAD = 8
HUB_COPY = 16
CHUNKS = 4
VM = pl.BlockSpec(memory_space=pltpu.VMEM)
ANY = pl.BlockSpec(memory_space=pl.ANY)
HBM = pl.BlockSpec(memory_space=pltpu.HBM)
BF, F32, I32 = jnp.bfloat16, jnp.float32, jnp.int32
vec = jax.ShapeDtypeStruct


def call(kernel, out_shape, in_specs, flops, bytes_accessed, limit=16, scratch=(), out_specs=None):
    single = not isinstance(out_shape, (list, tuple))
    return pl.pallas_call(
        kernel,
        out_shape=out_shape,
        in_specs=in_specs,
        out_specs=out_specs or (VM if single else [VM] * len(out_shape)),
        scratch_shapes=list(scratch),
        compiler_params=pltpu.CompilerParams(vmem_limit_bytes=limit << 20),
        cost_estimate=pl.CostEstimate(flops=4 * flops, bytes_accessed=bytes_accessed, transcendentals=0),
    )


def column_of(row, rows):
    return jnp.transpose(jnp.broadcast_to(row, (8, rows)))[:, :1]


def pick_matrix(rows_ref, shift, rows_here):
    me = lax.axis_index("member")
    caps = rows_ref.shape[1]
    wanted = column_of(rows_ref[pl.ds(me ^ shift, 1), :], caps)
    row_at = lax.broadcasted_iota(I32, (caps, rows_here), 1)
    return jnp.where(row_at == wanted, 1.0, 0.0).astype(BF)


def hub_matrix(hub_ref, rows_here):
    row_at = lax.broadcasted_iota(I32, (HUB_COPY, rows_here), 1)
    line = lax.broadcasted_iota(I32, (HUB_COPY, rows_here), 0)
    hit = jnp.zeros((HUB_COPY, rows_here), F32)
    for h in range(hub_ref.shape[0]):
        hit = hit + jnp.where((line == h) & (row_at == hub_ref[h]), 1.0, 0.0)
    return hit.astype(BF)


def load(small, feat_hbm, feat_ref, sems):
    copies = [pltpu.make_async_copy(a, b, sems.at[n]) for n, (a, b) in enumerate(small)]
    part = feat_ref.shape[0] // CHUNKS
    large = []
    for c in range(CHUNKS):
        span = pl.ds(c * part, part)
        large.append(pltpu.make_async_copy(feat_hbm.at[span, :], feat_ref.at[span, :], sems.at[len(small) + c]))
    for copy in copies + large:
        copy.start()
    for copy in copies:
        copy.wait()
    return large


def picked_rows(picks, feat_ref, copies):
    picks = jnp.concatenate(picks, axis=0)
    part = feat_ref.shape[0] // len(copies)
    picked = None
    for c, copy in enumerate(copies):
        copy.wait()
        span = slice(c * part, (c + 1) * part)
        term = jnp.dot(picks[:, span], feat_ref[span, :], preferred_element_type=F32)
        picked = term if picked is None else picked + term
    return picked.astype(BF)


def first_kernel(shifts, rows_hbm, hub_hbm, feat_hbm, *refs):
    outs, hub_out = refs[: len(shifts)], refs[len(shifts)]
    rows_ref, hub_ref, feat_ref, sems = refs[len(shifts) + 1 :]
    large = load([(rows_hbm, rows_ref), (hub_hbm, hub_ref)], feat_hbm, feat_ref, sems)
    rows_here = feat_ref.shape[0]
    caps = rows_ref.shape[1]
    picks = [pick_matrix(rows_ref, shift, rows_here) for shift in shifts]
    picked = picked_rows(picks + [hub_matrix(hub_ref, rows_here)], feat_ref, large)
    hubs = picked[len(shifts) * caps :]
    hub_out[...] = hubs
    for n in range(len(shifts)):
        block = picked[n * caps : (n + 1) * caps]
        outs[n][...] = jnp.concatenate([block, hubs[:HUB_PAD]], axis=0) if shifts[n] % 2 == 0 else block


def near_kernel(shifts, rows_hbm, hub_hbm, feat_hbm, after_ref, *refs):
    outs = refs[: len(shifts)]
    rows_ref, hub_ref, feat_ref, sems = refs[len(shifts) :]
    large = load([(rows_hbm, rows_ref), (hub_hbm, hub_ref)], feat_hbm, feat_ref, sems)
    caps = rows_ref.shape[1]
    picked = picked_rows([pick_matrix(rows_ref, shift, feat_ref.shape[0]) for shift in shifts], feat_ref, large)
    for n, shift in enumerate(shifts):
        block = picked[n * caps : (n + 1) * caps]
        outs[n][...] = jnp.concatenate([block, hub_ref[...][:HUB_PAD]], axis=0) if shift and shift % 2 == 0 else block


def rest_kernel(shifts, cols, rows_ref, feat_ref, after_ref, *outs):
    caps = rows_ref.shape[1]
    picks = [pick_matrix(rows_ref, shift, feat_ref.shape[0]) for shift in shifts]
    picked = jnp.dot(jnp.concatenate(picks, axis=0), feat_ref[:, cols], preferred_element_type=F32).astype(BF)
    for n in range(len(shifts)):
        outs[n][...] = picked[n * caps : (n + 1) * caps]


def join_kernel(spans, *refs):
    out_ref = refs[-1]
    at = 0
    for (start, stop), ref in zip(spans, refs):
        out_ref[at : at + stop - start, :] = ref[start:stop, :]
        at += stop - start


def add_counts(index, width, out_ref, row, column):
    rb, kmax = index.shape
    index = index.astype(jnp.int16)
    columns = [jnp.broadcast_to(index[:, k : k + 1], (rb, LANES)) for k in range(kmax)]
    lane = lax.broadcasted_iota(I32, (rb, LANES), 1).astype(jnp.int16)
    one = jnp.ones((rb, LANES), BF)
    zero = jnp.zeros((rb, LANES), BF)
    for g in range(width // LANES):
        number = lane + jnp.asarray(g * LANES, jnp.int16)
        total = zero
        for k in range(kmax):
            total = total + jnp.where(columns[k] == number, one, zero)
        out_ref[pl.ds(row, rb), column + g * LANES : column + (g + 1) * LANES] = total


def table_kernel(rb, peers, caps, hub_dev, magic, order, local_ref, hub_ref, halo_ref, deg_ref, after_ref, out_ref):
    me = lax.axis_index("member")
    group = lax.axis_index("group")
    rows_here = local_ref.shape[1]
    halo_slots = peers * caps
    hub_slots = out_ref.shape[1] - rows_here - halo_slots
    half = peers // 2

    def body(i, carry):
        row = pl.multiple_of(i * rb, rb)
        span = pl.ds(row, rb)

        def masked(which, index):
            slot = lax.broadcasted_iota(I32, index.shape, 0)
            return jnp.transpose(jnp.where(slot < deg_ref[which : which + 1, span], index, -1))

        local = masked(0, local_ref[:, span])
        hub = hub_ref[:, span]
        owner = (hub * magic) >> 16
        apart = (owner & (peers - 1)) ^ me
        line = (owner >> (peers.bit_length() - 1)) ^ group
        place = (apart & 1) * (hub_slots // (2 * HUB_PAD)) + line * half + (apart >> 1)
        hub = masked(1, place * HUB_PAD + hub - owner * hub_dev)
        slot = halo_ref[:, span]
        apart = (slot >> (caps.bit_length() - 1)) ^ me
        place = apart
        for n, shift in enumerate(order):
            if n != shift:
                place = jnp.where(apart == shift, n, place)
        halo = masked(2, place * caps + (slot & (caps - 1)))
        add_counts(local, rows_here, out_ref, row, 0)
        add_counts(halo, halo_slots, out_ref, row, rows_here)
        add_counts(hub, hub_slots, out_ref, row, rows_here + halo_slots)
        return carry

    lax.fori_loop(0, rows_here // rb, body, 0)


def own_kernel(rb, feat_ref, w_ref, bias_ref, after_ref, out_ref):
    bias = bias_ref[...].astype(F32)[None, :]
    for i in range(feat_ref.shape[0] // rb):
        span = pl.ds(i * rb, rb)
        out_ref[span, :] = jnp.dot(feat_ref[span, :], w_ref[...], preferred_element_type=F32) + bias


def local_kernel(rb, feat_ref, count_ref, after_ref, out_ref):
    rows_here = feat_ref.shape[0]
    for i in range(rows_here // rb):
        span = pl.ds(i * rb, rb)
        out_ref[span, :] = jnp.dot(count_ref[span, :rows_here], feat_ref[...], preferred_element_type=F32)


def sum_kernel(rb, sizes, at, sum_ref, count_ref, *refs):
    blocks, (_, out_ref, joined) = refs[: len(sizes)], refs[len(sizes) :]
    row = 0
    for size, ref in zip(sizes, blocks):
        joined[row : row + size, :] = ref[:size, :]
        row += size
    for i in range(sum_ref.shape[0] // rb):
        span = pl.ds(i * rb, rb)
        out_ref[span, :] = sum_ref[span, :] + jnp.dot(
            count_ref[span, at : at + row], joined[...], preferred_element_type=F32
        )


def means(at, cols, sum_ref, count_ref, deg_ref, block_ref, mean_ref):
    rb = 512
    for i in range(sum_ref.shape[0] // rb):
        span = pl.ds(i * rb, rb)
        deg = deg_ref[0:1, span] + deg_ref[1:2, span] + deg_ref[2:3, span]
        scale = column_of(1.0 / deg.astype(F32), rb)
        counts = count_ref[span, at : at + block_ref.shape[0]]
        total = sum_ref[span, cols] + jnp.dot(counts, block_ref[...], preferred_element_type=F32)
        mean_ref[span, :] = (total * scale).astype(BF)


def late_kernel(rb, at, cols, own_ref, sum_ref, count_ref, deg_ref, w_ref, block_ref, out_ref, mean_ref):
    means(at, cols, sum_ref, count_ref, deg_ref, block_ref, mean_ref)
    for i in range(sum_ref.shape[0] // rb):
        span = pl.ds(i * rb, rb)
        out_ref[span, :] = own_ref[span, :] + jnp.dot(mean_ref[span, :], w_ref[cols, :], preferred_element_type=F32)


def last_kernel(rb, at, cols, own_ref, sum_ref, count_ref, deg_ref, w_ref, block_ref, out_hbm, mean_ref, out_ref, sems):
    means(at, cols, sum_ref, count_ref, deg_ref, block_ref, mean_ref)
    copies = []
    for i in range(sum_ref.shape[0] // rb):
        span = pl.ds(i * rb, rb)
        value = own_ref[span, :] + jnp.dot(mean_ref[span, :], w_ref[cols, :], preferred_element_type=F32)
        out_ref[span, :] = jnp.maximum(value, 0.0).astype(BF)
        copies.append(pltpu.make_async_copy(out_ref.at[span, :], out_hbm.at[span, :], sems.at[i]))
        copies[-1].start()
    for copy in copies:
        copy.wait()


def per_device(groups, features, w_self, w_neigh, bias, hub_rows, hub_nbrs, local_nbrs, halo_nbrs, degrees, send_rows):
    rows_here, width = features.shape
    peers, caps = send_rows.shape[1:]
    hub_dev = hub_rows.shape[0]
    magic = -(-(1 << 16) // hub_dev)
    assert all((h * magic) >> 16 == h // hub_dev for h in range(hub_dev * peers * groups))
    assert peers >= 8 and groups >= 4 and hub_dev <= HUB_PAD
    assert not any(n & (n - 1) for n in (peers, groups, caps))
    rows = send_rows.reshape(peers, caps)
    hub_slots = HUB_PAD * peers * groups

    top, last = peers // 2, peers - 1
    far = [last - 1]
    near = list(range(top, last - 1, 2)) + list(range(2, top, 2))
    other = list(range(3, last, 2))
    early = [0, 1] + near + far
    order = early + [last] + other
    cuts = [0, width // 2, 3 * width // 4, width]
    spans = [slice(a, b) for a, b in zip(cuts, cuts[1:])]

    def swap(block, axis, shift):
        size = peers if axis == "member" else groups
        return lax.ppermute(block, axis, [(i, i ^ shift) for i in range(size)])

    scratch = [pltpu.VMEM((rows_here, width), BF), pltpu.SemaphoreType.DMA((2 + CHUNKS,))]
    plain, carrier = vec((caps, width), BF), vec((caps + HUB_PAD, width), BF)
    firsts = call(
        functools.partial(first_kernel, far + [1]),
        [carrier] * len(far) + [plain, vec((HUB_COPY, width), BF)],
        [HBM] * 3,
        0,
        2 * rows_here * width,
        limit=60,
        scratch=[pltpu.VMEM((peers, caps), I32), pltpu.SMEM((hub_dev,), I32)] + scratch,
    )(rows, hub_rows, features)
    hubs = firsts[-1]
    got = {shift: swap(block, "member", shift) for shift, block in zip(far + [1], firsts)}
    nears = call(
        functools.partial(near_kernel, near + [0]),
        [plain if shift % 2 else carrier for shift in near] + [plain],
        [HBM] * 3 + [ANY],
        0,
        2 * rows_here * width,
        limit=60,
        scratch=[pltpu.VMEM((peers, caps), I32), pltpu.VMEM((HUB_COPY, width), BF)] + scratch,
    )(rows, hubs, features, got[1])
    for shift, block in zip(near, nears):
        got[shift] = swap(block, "member", shift)
    got[0] = nears[-1]

    counts = call(
        functools.partial(table_kernel, 2 * LANES, peers, caps, hub_dev, magic, order),
        vec((rows_here, rows_here + peers * caps + hub_slots), BF),
        [VM] * 4 + [ANY],
        24 * rows_here * (rows_here + peers * caps),
        2 * rows_here * (rows_here + hub_slots + peers * caps),
    )(local_nbrs.T, hub_nbrs.T, halo_nbrs.T, degrees, got[0])

    def rest(shifts, cols, after, weight=1):
        return call(
            functools.partial(rest_kernel, shifts, cols),
            [vec((caps, cols.stop - cols.start), BF)] * len(shifts),
            [VM] * 2 + [ANY],
            weight * 2 * len(shifts) * caps * rows_here * width,
            2 * rows_here * width,
        )(rows, features, after)

    def join(blocks, spans, after):
        total = sum(stop - start for start, stop in spans)
        return call(
            functools.partial(join_kernel, spans),
            vec((total, width), BF),
            [VM] * len(blocks) + [ANY],
            0,
            4 * total * width,
            limit=4,
        )(*blocks, after)

    def add(total, blocks, sizes, at, after, weight=1):
        return call(
            functools.partial(sum_kernel, 512, sizes, at),
            vec((rows_here, width), F32),
            [VM] * (2 + len(blocks)) + [ANY],
            weight * 2 * rows_here * width * sum(sizes),
            8 * rows_here * width,
            scratch=[pltpu.VMEM((sum(sizes), width), BF)],
        )(total, counts, *blocks, after)

    own = call(
        functools.partial(own_kernel, 512),
        vec((rows_here, width), F32),
        [VM] * 3 + [ANY],
        2 * rows_here * width * width,
        8 * rows_here * width,
    )(features, w_self, bias, counts)
    total = call(
        functools.partial(local_kernel, 512),
        vec((rows_here, width), F32),
        [VM] * 2 + [ANY],
        2 * rows_here * rows_here * width,
        8 * rows_here * width,
    )(features, counts, own)
    odd = rest(other, slice(0, width), total)
    for shift, block in zip(other, odd):
        got[shift] = swap(block, "member", shift)

    evens = [got[s] for s in range(2, peers, 2)]
    hubs = join([hubs, *evens], [(0, HUB_PAD)] + [(caps, caps + HUB_PAD)] * len(evens), odd[0])
    lines = [swap(hubs, "group", shift) for shift in range(1, groups)]
    late = rest([last], spans[0], hubs, 32)
    hubs = join([hubs, *lines], [(0, hubs.shape[0])] * groups, late[0])
    other_hubs = swap(hubs, "member", 1)
    total = add(total, [got[s] for s in early], [caps] * len(early), rows_here, hubs, 16)
    total = add(total, [hubs, other_hubs], [hub_slots // 2] * 2, rows_here + caps * peers, total)
    late += rest([last], spans[1], total)
    at = rows_here + caps * order.index(other[0])
    total = add(total, [got[s] for s in other], [caps] * len(other), at, total)
    late += rest([last], spans[2], total)
    late = [swap(block, "member", last) for block in late]

    at = rows_here + caps * order.index(last)
    value = own
    for span, block in zip(spans[:-1], late):
        value = call(
            functools.partial(late_kernel, 512, at, span),
            vec((rows_here, width), F32),
            [VM] * 6,
            2 * rows_here * (span.stop - span.start) * width,
            8 * rows_here * width,
            scratch=[pltpu.VMEM((rows_here, span.stop - span.start), BF)],
        )(value, total, counts, degrees, w_neigh, block)
    return call(
        functools.partial(last_kernel, 256, at, spans[-1]),
        vec((rows_here, width), BF),
        [VM] * 6,
        2 * rows_here * (width - spans[-1].start) * width,
        8 * rows_here * width,
        scratch=[
            pltpu.VMEM((rows_here, width - spans[-1].start), BF),
            pltpu.VMEM((rows_here, width), BF),
            pltpu.SemaphoreType.DMA((rows_here // 256,)),
        ],
        out_specs=ANY,
    )(value, total, counts, degrees, w_neigh, late[-1])


def solution(mesh):
    both = ("group", "member")
    in_specs = (
        P(both, None),
        P(),
        P(),
        P(),
        P(both),
        P(both, None),
        P(both, None),
        P(both, None),
        P(None, both),
        P(both, None, None),
    )
    return jax.shard_map(
        functools.partial(per_device, mesh.shape["group"]),
        mesh=mesh,
        in_specs=in_specs,
        out_specs=P(both, None),
        check_vma=False,
    )
```
